256 devices in a mesh: view: 16 (over x_lo, z), seq: 16 (over y, x_hi, core).
Axes of the slice: x: 4 (x_hi: 2, x_lo: 2; x = x_hi * 2 + x_lo), y: 4, z: 8, core: 2. Of those that a mesh axis runs over, the one named last changes fastest.
Arguments:
- tokens: bfloat16 [16, 6144, 1024], P('view', 'seq'), may hold values from -6 to 6
- w_cross_qkv: bfloat16 [1024, 3072], replicated, may hold values from -8 to 8
- w_cross_out: bfloat16 [1024, 1024], replicated, may hold values from -3 to 3
- w_temporal_qkv: bfloat16 [1024, 3072], P('view'), may hold values from -8 to 8
- w_temporal_out: bfloat16 [1024, 1024], P('view'), may hold values from -0.359375 to 0.359375
Outputs:
- cross_update: bfloat16 [16, 6144, 1024], P('view', 'seq')
- temporal_update: bfloat16 [16, 6144, 1024], P('view', 'seq')
The draws below stay inside these ranges and needn't reach their ends.
All inputs are finite; a program needn't handle non-finite values.
Results may differ from the reference program's by a relative error of at most 0.02.
Values may be sent and summed in bfloat16 or wider, within the bound.
No kernel may reach another device: no remote copies, remote signals or barrier semaphores. Data moves between devices by JAX's collectives and lax.ppermute only.
A program may use at most 128 MiB of HBM per device.

```python
import jax
import jax.numpy as jnp
from jax import lax

D = 1024
HEADS = 16
HD = 64
SPATIAL = 768
FRAMES = 8
TOKENS_VIEW = 6144
VIEWS = 16


def independent_columns(key):
    query_key, keys_key, value_key = jax.random.split(key, 3)
    factor = D ** (-0.5)
    query_part = jnp.clip(jax.random.normal(query_key, (D, D), jnp.float32), -4.0, 4.0) * factor
    keys_part = jnp.clip(jax.random.normal(keys_key, (D, D), jnp.float32), -4.0, 4.0) * factor
    value_part = jnp.clip(jax.random.normal(value_key, (D, D), jnp.float32), -4.0, 4.0) * factor
    return (query_part, keys_part, value_part)


def draw_tokens(key, part):
    key = jax.random.fold_in(key, 5)
    first_key = jax.random.fold_in(key, 0)
    drawn = jax.random.normal(first_key, (VIEWS, TOKENS_VIEW, D), jnp.float32)
    return jnp.clip(drawn, -6.0, 6.0).astype(jnp.bfloat16)


def draw_w_cross_qkv(key, part):
    key = jax.random.fold_in(key, 11)
    first_key = jax.random.fold_in(key, 0)
    query_part, keys_part, value_part = independent_columns(first_key)
    return jnp.concatenate([query_part, keys_part, value_part], 1).astype(jnp.bfloat16)


def draw_w_temporal_qkv(key, part):
    key = jax.random.fold_in(key, 23)
    first_key = jax.random.fold_in(key, 0)
    query_part, keys_part, value_part = independent_columns(first_key)
    return jnp.concatenate([query_part, keys_part, value_part], 1).astype(jnp.bfloat16)


def level_of(key, dims, cuts, low, largest):
    factor_of = 1.0
    for position, parts in cuts:
        heights = jax.random.uniform(jax.random.fold_in(jax.random.fold_in(key, 6), position), (parts,), jnp.float32, low / len(cuts), largest / len(cuts))
        factor_of = factor_of * jnp.repeat(jnp.exp(heights), dims[position] // parts).reshape((-1,) + (1,) * (len(dims) - 1 - position))
    return factor_of


def normal_values(rng, dims, deviation, bound, pieces=(), kind=jnp.bfloat16):
    gain = level_of(rng, dims, pieces, -0.22, 0.18) if pieces else 1.0
    array = jax.random.normal(rng, dims, jnp.float32) * deviation * gain
    return jnp.minimum(jnp.maximum(array, -bound), bound).astype(kind)


def setup_inputs(seed: int = 0) -> dict:
    key_of = jax.random.split(jax.random.key(seed), 6)
    tokens = draw_tokens(jax.random.fold_in(key_of[5], 71), 0)
    w_cross_qkv = draw_w_cross_qkv(jax.random.fold_in(key_of[5], 71), 0)
    w_cross_out = normal_values(key_of[2], (D, D), 0.5, 3.0)
    w_temporal_qkv = draw_w_temporal_qkv(jax.random.fold_in(key_of[5], 71), 0)
    w_temporal_out = normal_values(key_of[4], (D, D), 0.06, 0.359375, ((0, 16),))
    return {"tokens": tokens, "w_cross_qkv": w_cross_qkv, "w_cross_out": w_cross_out, "w_temporal_qkv": w_temporal_qkv, "w_temporal_out": w_temporal_out}


def layer_norm(inputs):
    widened = inputs.astype(jnp.float32)
    average = lax.optimization_barrier(jnp.mean(widened, axis=-1, keepdims=True))
    centred = widened - average
    variance = lax.optimization_barrier(jnp.mean(centred * centred, axis=-1, keepdims=True))
    return (centred * lax.rsqrt(variance + 1e-06)).astype(jnp.bfloat16)

def cross_attend(queries, keys_all, values_all):
    scores = jnp.einsum('tha,sha->hts', queries.astype(jnp.float32), keys_all.astype(jnp.float32)) * HD ** (-0.5)
    row_peak = lax.optimization_barrier(jnp.max(scores, axis=-1, keepdims=True))
    weights = jnp.exp(scores - row_peak)
    totals = lax.optimization_barrier(jnp.sum(weights, axis=-1))
    rounded = lax.optimization_barrier(weights.astype(jnp.bfloat16))
    result = jnp.einsum('hts,sha->tha', rounded.astype(jnp.float32), values_all.astype(jnp.float32))
    return (result / jnp.transpose(totals)[:, :, None]).astype(jnp.bfloat16)

def temporal_attend(queries, keys_all, values_all):
    scores = jnp.einsum('fsha,gsha->shfg', queries.astype(jnp.float32), keys_all.astype(jnp.float32)) * HD ** (-0.5)
    row_peak = lax.optimization_barrier(jnp.max(scores, axis=-1, keepdims=True))
    weights = jnp.exp(scores - row_peak)
    totals = lax.optimization_barrier(jnp.sum(weights, axis=-1))
    rounded = lax.optimization_barrier(weights.astype(jnp.bfloat16))
    result = jnp.einsum('shfg,gsha->fsha', rounded.astype(jnp.float32), values_all.astype(jnp.float32))
    return (result / jnp.transpose(totals, (2, 0, 1))[..., None]).astype(jnp.bfloat16)

def reference(tokens, w_cross_qkv, w_cross_out, w_temporal_qkv, w_temporal_out):
    normed = layer_norm(tokens)
    projected = jnp.dot(normed.reshape(VIEWS * TOKENS_VIEW, D), w_cross_qkv, preferred_element_type=jnp.float32).astype(jnp.bfloat16)
    projected = projected.reshape(VIEWS, FRAMES, SPATIAL, 3, HEADS, HD)

    def per_view(view_index):
        current = projected[view_index]
        previous = projected[(view_index + VIEWS - 1) % VIEWS]
        following = projected[(view_index + 1) % VIEWS]

        def per_frame(frame_index):
            queries = current[frame_index, :, 0]
            keys_all = jnp.concatenate([previous[frame_index, :, 1], current[frame_index, :, 1], following[frame_index, :, 1]], 0)
            values_all = jnp.concatenate([previous[frame_index, :, 2], current[frame_index, :, 2], following[frame_index, :, 2]], 0)
            return cross_attend(queries, keys_all, values_all)
        return lax.map(per_frame, jnp.arange(FRAMES, dtype=jnp.int32))
    attended = lax.map(per_view, jnp.arange(VIEWS, dtype=jnp.int32))
    cross_update = jnp.dot(attended.reshape(VIEWS * TOKENS_VIEW, D), w_cross_out, preferred_element_type=jnp.float32).astype(jnp.bfloat16)
    cross_update = cross_update.reshape(VIEWS, TOKENS_VIEW, D)
    residual = tokens.astype(jnp.float32) + cross_update.astype(jnp.float32)
    normed_two = layer_norm(residual)
    temporal = jnp.dot(normed_two.reshape(VIEWS * TOKENS_VIEW, D), w_temporal_qkv, preferred_element_type=jnp.float32).astype(jnp.bfloat16)
    temporal = temporal.reshape(VIEWS, FRAMES, SPATIAL, 3, HEADS, HD)

    def temporal_view(view_block):
        return temporal_attend(view_block[:, :, 0], view_block[:, :, 1], view_block[:, :, 2])
    mixed_heads = lax.map(temporal_view, temporal)
    temporal_update = jnp.dot(mixed_heads.reshape(VIEWS * TOKENS_VIEW, D), w_temporal_out, preferred_element_type=jnp.float32).astype(jnp.bfloat16)
    return (cross_update, temporal_update.reshape(VIEWS, TOKENS_VIEW, D))
```

```python
import functools

import jax
import jax.numpy as jnp
from jax import lax
from jax.experimental import pallas as pl
from jax.experimental.pallas import tpu as pltpu
from jax.sharding import Mesh
from jax.sharding import PartitionSpec as P

HEADS = 16
HD = 64
PAIR = 2 * HD
QUAD = 4 * HD
LOG2E = 1.4426950408889634
VMEM_LIMIT = 56 * 1024 * 1024
F32 = jnp.float32
BF16 = jnp.bfloat16


def dot(a, b):
    return jnp.dot(a, b, preferred_element_type=F32)


def layer_norm(rows):
    centred = rows - jnp.mean(rows, axis=-1, keepdims=True)
    variance = jnp.mean(centred * centred, axis=-1, keepdims=True)
    return (centred * lax.rsqrt(variance + 1e-06)).astype(BF16)


def lanes_of(width, index, rows=1):
    lane = lax.broadcasted_iota(jnp.int32, (rows, width), 1)
    return jnp.where(lane // HD == index, 1.0, 0.0).astype(BF16)


def cross_step_kernel(first, last, row_block, *refs):
    refs = list(refs)
    refs.pop(0)
    x_refs = [refs.pop(0), refs.pop(0)]
    if first:
        wq_ref = refs.pop(0)
    wk_ref, wv_ref = refs.pop(0), refs.pop(0)
    if not first:
        q_ref, o_in, m_in, l_in = (refs.pop(0) for _ in range(4))
    if first:
        q_ref = refs.pop(0)
    if last:
        halves = [refs.pop(0), refs.pop(0)]
    else:
        o_out, m_out, l_out = (refs.pop(0) for _ in range(3))
    norm_s, kt_s, v_s = refs
    half = x_refs[0].shape[0]
    keys = 2 * half
    pairs = kt_s.shape[0]
    step = pl.program_id(0)

    @pl.when(step == 0)
    def _():
        for part, x_ref in enumerate(x_refs):
            norm_s[part * half : (part + 1) * half, :] = layer_norm(x_ref[...].astype(F32))
        normed = norm_s[...]
        if first:
            queries = (dot(normed, wq_ref[...]) * (HD**-0.5 * LOG2E)).astype(BF16)
            for pair in range(pairs):
                q_ref[pair] = queries[:, pair * PAIR : (pair + 1) * PAIR]
        made_keys = dot(normed, wk_ref[...]).astype(BF16)
        made_values = dot(normed, wv_ref[...]).astype(BF16)
        for pair in range(pairs):
            kt_s[pair] = made_keys[:, pair * PAIR : (pair + 1) * PAIR].T
            v_s[pair, :, :PAIR] = made_values[:, pair * PAIR : (pair + 1) * PAIR]
            v_s[pair, :, PAIR:] = jnp.ones((keys, PAIR), BF16)

    index = step if first else 0
    transposed, values = kt_s[step], v_s[step]
    low = lax.broadcasted_iota(jnp.int32, (row_block, PAIR), 1) < HD
    for start in range(0, keys, row_block):
        rows = slice(start, start + row_block)
        queries = q_ref[index, rows, :]
        peaks, sums = [], []
        for head in range(2):
            scores = dot(queries * lanes_of(PAIR, head), transposed)
            peak = jnp.max(scores, axis=-1, keepdims=True)
            if not first:
                peak = jnp.maximum(peak, m_in[0, rows, head * HD : head * HD + 1])
            weights = jnp.exp2(scores - peak).astype(BF16)
            peaks.append(peak)
            sums.append(dot(weights, values))
        peak = jnp.where(low, peaks[0], peaks[1])
        result = jnp.where(low, sums[0][:, :PAIR], sums[1][:, :PAIR])
        total = jnp.where(low, sums[0][:, PAIR:], sums[1][:, PAIR:])
        if not first:
            scale = jnp.exp2(m_in[0, rows, :] - peak)
            result = result + scale * o_in[0, rows, :]
            total = total + scale * l_in[0, rows, :]
        if last:
            part, offset = divmod(start, half)
            halves[part][offset : offset + row_block, :] = (result / total).astype(BF16)
        else:
            o_out[0, rows, :] = result
            m_out[0, rows, :] = peak
            l_out[0, rows, :] = total


def cross_step(core, xs, w_cross_qkv, state=None, last=False, row_block=384):
    first = state is None
    half, features = xs[0].shape
    keys = 2 * half
    columns = features // 2
    pairs = columns // PAIR
    whole = pl.BlockSpec((half, features), lambda p, c: (0, 0))
    column = lambda which: pl.BlockSpec((features, columns), lambda p, c: (0, 2 * which + c[0]))
    by_pair = pl.BlockSpec((1, keys, PAIR), lambda p, c: (p, 0, 0))
    all_pairs = pl.BlockSpec((pairs, keys, PAIR), lambda p, c: (0, 0, 0))
    kept = jax.ShapeDtypeStruct((pairs, keys, PAIR), F32)
    in_specs = [whole, whole] + [column(which) for which in ((0, 1, 2) if first else (1, 2))]
    operands = list(xs) + [w_cross_qkv] * (3 if first else 2)
    out_specs, out_shape = [], []
    if first:
        out_specs.append(all_pairs)
        out_shape.append(jax.ShapeDtypeStruct((pairs, keys, PAIR), BF16))
    else:
        in_specs += [by_pair] * 4
        operands += list(state)
    if last:
        out_specs += [pl.BlockSpec((half, PAIR), lambda p, c: (0, p))] * 2
        out_shape += [jax.ShapeDtypeStruct((half, columns), BF16)] * 2
    else:
        out_specs += [by_pair] * 3
        out_shape += [kept] * 3
    flops = 2 * keys * features * columns * (3 if first else 2) + 16 * keys * keys * PAIR * pairs
    return pl.pallas_call(
        functools.partial(cross_step_kernel, first, last, row_block),
        grid_spec=pltpu.PrefetchScalarGridSpec(
            num_scalar_prefetch=1,
            grid=(pairs,),
            in_specs=in_specs,
            out_specs=out_specs,
            scratch_shapes=[
                pltpu.VMEM((keys, features), BF16),
                pltpu.VMEM((pairs, PAIR, keys), BF16),
                pltpu.VMEM((pairs, keys, 2 * PAIR), BF16),
            ],
        ),
        out_shape=out_shape,
        compiler_params=pltpu.CompilerParams(vmem_limit_bytes=VMEM_LIMIT),
        cost_estimate=pl.CostEstimate(
            flops=flops, bytes_accessed=12 * 2**20, transcendentals=2 * keys * keys * pairs
        ),
        name="cross_first" if first else "cross_last" if last else "cross_middle",
    )(core, *operands)


def cross_out_kernel(core_ref, mine_ref, other_ref, x_ref, wm_ref, wo_ref, cross_ref, norm_ref):
    made = dot(mine_ref[...], wm_ref[...]) + dot(other_ref[...], wo_ref[...])
    cross_ref[...] = made.astype(BF16)
    residual = x_ref[...].astype(F32) + cross_ref[...].astype(F32)
    norm_ref[...] = layer_norm(residual)


def cross_out(core, mine, other, tokens, w_cross_out):
    rows, features = tokens.shape
    whole = lambda shape: pl.BlockSpec(shape, lambda s, c: (0, 0))
    half = features // 2
    return pl.pallas_call(
        cross_out_kernel,
        grid_spec=pltpu.PrefetchScalarGridSpec(
            num_scalar_prefetch=1,
            grid=(1,),
            in_specs=[
                whole((rows, half)),
                whole((rows, half)),
                whole((rows, features)),
                pl.BlockSpec((half, features), lambda s, c: (c[0], 0)),
                pl.BlockSpec((half, features), lambda s, c: (1 - c[0], 0)),
            ],
            out_specs=[whole((rows, features))] * 2,
        ),
        out_shape=[jax.ShapeDtypeStruct((rows, features), BF16)] * 2,
        compiler_params=pltpu.CompilerParams(vmem_limit_bytes=VMEM_LIMIT),
        cost_estimate=pl.CostEstimate(
            flops=2 * rows * features * features, bytes_accessed=6 * 2**20, transcendentals=0
        ),
        name="cross_out",
    )(core, mine, other, tokens, w_cross_out, w_cross_out)


GROUP = 16


def temporal_kernel(core_ref, x_ref, *refs):
    mine_refs, other_refs = refs[:3], refs[3:6]
    wo_ref, out_ref, x_s, att_s, acc_s = refs[6:]
    frames, positions, _ = x_ref.shape
    groups = positions // GROUP
    size = frames * GROUP
    step = pl.program_id(0)

    @pl.when(step == 0)
    def _():
        for group in range(groups):
            for frame in range(frames):
                x_s[pl.ds(group * size + frame * GROUP, GROUP), :] = x_ref[
                    frame, group * GROUP : (group + 1) * GROUP, :
                ]

    def attend(w_refs):
        rows = x_s[...]
        queries = (dot(rows, w_refs[0][...]) * (HD**-0.5 * LOG2E)).astype(BF16)
        keys = dot(rows, w_refs[1][...]).astype(BF16)
        values = dot(rows, w_refs[2][...]).astype(BF16)
        row = lax.broadcasted_iota(jnp.int32, (size, size), 0)
        column = lax.broadcasted_iota(jnp.int32, (size, size), 1)
        same = row % GROUP == column % GROUP
        head_of = lax.broadcasted_iota(jnp.int32, (size, QUAD), 1) // HD
        for group in range(groups):
            part = slice(group * size, (group + 1) * size)
            transposed = keys[part].T
            attended = jnp.zeros((size, QUAD), F32)
            for head in range(QUAD // HD):
                scores = dot(queries[part] * lanes_of(QUAD, head), transposed)
                scores = jnp.where(same, scores, -jnp.inf)
                weights = jnp.exp2(scores - jnp.max(scores, axis=-1, keepdims=True))
                total = jnp.sum(weights, axis=-1, keepdims=True)
                result = dot(weights.astype(BF16), values[part]) / total
                attended = jnp.where(head_of == head, result, attended)
            att_s[part, :] = attended.astype(BF16)

    half_steps = pl.num_programs(0) // 2

    @pl.when(step < half_steps)
    def _():
        attend(mine_refs)

    @pl.when(step >= half_steps)
    def _():
        attend(other_refs)

    made = dot(att_s[...], wo_ref[...])

    @pl.when(step == 0)
    def _():
        acc_s[...] = made

    @pl.when(step > 0)
    def _():
        acc_s[...] += made

    @pl.when(step == pl.num_programs(0) - 1)
    def _():
        for group in range(groups):
            for frame in range(frames):
                out_ref[frame, group * GROUP : (group + 1) * GROUP, :] = acc_s[
                    pl.ds(group * size + frame * GROUP, GROUP), :
                ].astype(BF16)


def temporal(core, rows, mine, other, w_out):
    frames, positions, features = rows.shape
    count = frames * positions
    steps = features // QUAD
    whole = pl.BlockSpec((frames, positions, features), lambda j, c: (0, 0, 0))

    def column(which, own):
        def index(j, c):
            inside = jnp.minimum(j, 1) if own else jnp.maximum(j - 2, 0)
            return (0, 2 * which + inside)

        return pl.BlockSpec((features, QUAD), index)

    def out_rows(j, c):
        return (jnp.where(j < 2, 2 * c[0] + j, 2 * (1 - c[0]) + j - 2), 0)

    return pl.pallas_call(
        temporal_kernel,
        grid_spec=pltpu.PrefetchScalarGridSpec(
            num_scalar_prefetch=1,
            grid=(steps,),
            in_specs=[whole]
            + [column(which, True) for which in range(3)]
            + [column(which, False) for which in range(3)]
            + [pl.BlockSpec((QUAD, features), out_rows)],
            out_specs=whole,
            scratch_shapes=[
                pltpu.VMEM((count, features), BF16),
                pltpu.VMEM((count, QUAD), BF16),
                pltpu.VMEM((count, features), F32),
            ],
        ),
        out_shape=jax.ShapeDtypeStruct(rows.shape, BF16),
        compiler_params=pltpu.CompilerParams(vmem_limit_bytes=VMEM_LIMIT),
        cost_estimate=pl.CostEstimate(
            flops=8 * count * features * features, bytes_accessed=10 * 2**20, transcendentals=0
        ),
        name="temporal",
    )(core, rows, mine, mine, mine, other, other, other, w_out)


VIEW = ("xl", "z")
FRAME = ("y", "xh")
SWAP = [(0, 1), (1, 0)]


def per_device(tokens, w_cross_qkv, w_cross_out, w_temporal_qkv, w_temporal_out):
    own = tokens[0]
    rows, features = own.shape
    half = features // 2
    core_index = lax.axis_index("c")
    core = core_index.astype(jnp.int32).reshape(1)
    views = lax.axis_size(VIEW)
    forward = [(i, (i + 1) % views) for i in range(views)]
    backward = [(i, (i - 1) % views) for i in range(views)]

    partner = lax.ppermute(own, "c", SWAP)
    before = lax.ppermute(own, VIEW, forward)
    after = lax.ppermute(own, VIEW, backward)

    shard = w_temporal_qkv.reshape(-1, 3, 2, half)
    shard = lax.dynamic_index_in_dim(shard, core_index, 2, keepdims=False).reshape(-1, 3 * half)
    w_mine = lax.all_gather(shard, VIEW, axis=0, tiled=True)
    w_other = lax.ppermute(w_mine, "c", SWAP)
    w_out = lax.all_gather(w_temporal_out, VIEW, axis=0, tiled=True)

    state = cross_step(core, (own, partner), w_cross_qkv)
    before_other = lax.ppermute(before, "c", SWAP)
    after_other = lax.ppermute(after, "c", SWAP)
    state = (state[0],) + tuple(cross_step(core, (before, after), w_cross_qkv, state))
    mine, theirs = cross_step(core, (before_other, after_other), w_cross_qkv, state, last=True)
    other = lax.ppermute(theirs, "c", SWAP)
    cross_rows, normed = cross_out(core, mine, other, own, w_cross_out)

    frames = lax.axis_size(FRAME)
    spread = lax.all_to_all(normed, FRAME, split_axis=0, concat_axis=0, tiled=True)
    updated = temporal(
        core, spread.reshape(frames, rows // frames, features), w_mine, w_other, w_out
    )
    temporal_rows = lax.all_to_all(
        updated.reshape(rows, features), FRAME, split_axis=0, concat_axis=0, tiled=True
    )
    return (cross_rows[None], temporal_rows[None])


def solution(mesh):
    fine = Mesh(mesh.devices.reshape(2, 8, 4, 2, 2), ("xl", "z", "y", "xh", "c"))
    by_token = P(VIEW, FRAME + ("c",), None)
    placed = (by_token, P(), P(), P(VIEW, None), P(VIEW, None))
    return jax.shard_map(
        per_device,
        mesh=fine,
        in_specs=placed,
        out_specs=(by_token, by_token),
        check_vma=False,
    )
```

```python
import functools

import jax
import jax.numpy as jnp
from jax import lax
from jax.experimental import pallas as pl
from jax.experimental.pallas import tpu as pltpu
from jax.sharding import Mesh
from jax.sharding import PartitionSpec as P

HEADS = 16
HD = 64
PAIR = 2 * HD
QUAD = 4 * HD
LOG2E = 1.4426950408889634
CROSS_LIMIT = 24 * 1024 * 1024
UNROLL = 4
F32 = jnp.float32
BF16 = jnp.bfloat16


def dot(a, b):
    return jnp.dot(a, b, preferred_element_type=F32)


def layer_norm(rows):
    centred = rows - jnp.mean(rows, axis=-1, keepdims=True)
    variance = jnp.mean(centred * centred, axis=-1, keepdims=True)
    return (centred * lax.rsqrt(variance + 1e-06)).astype(BF16)


def lanes_of(width, index, rows=1):
    lane = lax.broadcasted_iota(jnp.int32, (rows, width), 1)
    return jnp.where(lane // HD == index, 1.0, 0.0).astype(BF16)


def cross_step_kernel(first, last, blocks, row_block, *refs):
    refs = list(refs)
    take = lambda count: [refs.pop(0) for _ in range(count)]
    x_refs = take(blocks)
    w_refs = take(3 if first else 2)
    if first:
        (q_ref,) = take(1)
    else:
        q_ref, o_in, m_in, l_in = take(4)
    if last:
        halves = take(2)
    else:
        o_out, m_out, l_out = take(3)
    norm_s, kt_s, v_s = refs
    pairs, count = q_ref.shape[:2]
    keys = kt_s.shape[2]

    start = 0
    for x_ref in x_refs:
        norm_s[start : start + x_ref.shape[0], :] = layer_norm(x_ref[...].astype(F32))
        start += x_ref.shape[0]

    def project(which, quad):
        return dot(norm_s[...], w_refs[which][:, quad * QUAD : (quad + 1) * QUAD])

    for quad in range(pairs // 2):
        if first:
            made = (project(2, quad) * (HD**-0.5 * LOG2E)).astype(BF16)
            for part in range(2):
                q_ref[2 * quad + part] = made[:, part * PAIR : (part + 1) * PAIR]
        made = project(0, quad).astype(BF16)
        for part in range(2):
            kt_s[2 * quad + part] = made[:, part * PAIR : (part + 1) * PAIR].T
        made = project(1, quad).astype(BF16)
        for part in range(2):
            v_s[2 * quad + part, :, :PAIR] = made[:, part * PAIR : (part + 1) * PAIR]
            v_s[2 * quad + part, :, PAIR:] = jnp.ones((keys, PAIR), BF16)

    low = lax.broadcasted_iota(jnp.int32, (row_block, PAIR), 1) < HD

    def attend(pair, carry):
        transposed, values = kt_s[pair], v_s[pair]
        for start in range(0, count, row_block):
            rows = slice(start, start + row_block)
            queries = q_ref[pair, rows, :]
            peaks, sums = [], []
            for head in range(2):
                scores = dot(queries * lanes_of(PAIR, head), transposed)
                peak = jnp.max(scores, axis=-1, keepdims=True)
                weights = jnp.exp2(scores - peak).astype(BF16)
                peaks.append(peak)
                sums.append(dot(weights, values))
            peak = jnp.where(low, peaks[0], peaks[1])
            result = jnp.where(low, sums[0][:, :PAIR], sums[1][:, :PAIR])
            total = jnp.where(low, sums[0][:, PAIR:], sums[1][:, PAIR:])
            if not first:
                highest = jnp.maximum(peak, m_in[pair, rows, :])
                old, new = jnp.exp2(m_in[pair, rows, :] - highest), jnp.exp2(peak - highest)
                result = new * result + old * o_in[pair, rows, :]
                total = new * total + old * l_in[pair, rows, :]
                peak = highest
            if last:
                half = count // 2
                part, offset = divmod(start, half)
                halves[part][pair, offset : offset + row_block, :] = (result / total).astype(BF16)
            else:
                o_out[pair, rows, :] = result
                m_out[pair, rows, :] = peak
                l_out[pair, rows, :] = total
        return carry

    lax.fori_loop(0, pairs, attend, 0, unroll=UNROLL)


VMEM_SPEC = pl.BlockSpec(memory_space=pltpu.VMEM)
SMEM_SPEC = pl.BlockSpec(memory_space=pltpu.SMEM)


def cross_step(xs, weights, state=None, last=False, row_block=384):
    first = state is None
    features, columns = weights[0].shape
    keys = sum(x.shape[0] for x in xs)
    pairs = columns // PAIR
    count = keys if first else state[0].shape[1]
    kept = jax.ShapeDtypeStruct((pairs, count, PAIR), F32)
    operands = list(xs) + list(weights)
    out_shape = []
    if first:
        out_shape.append(jax.ShapeDtypeStruct((pairs, count, PAIR), BF16))
    else:
        operands += list(state)
    if last:
        out_shape += [jax.ShapeDtypeStruct((pairs, count // 2, PAIR), BF16)] * 2
    else:
        out_shape += [kept] * 3
    flops = 2 * keys * features * columns * len(weights) + 16 * count * keys * PAIR * pairs
    return pl.pallas_call(
        functools.partial(cross_step_kernel, first, last, len(xs), row_block),
        in_specs=[VMEM_SPEC] * len(operands),
        out_specs=[VMEM_SPEC] * len(out_shape),
        scratch_shapes=[
            pltpu.VMEM((keys, features), BF16),
            pltpu.VMEM((pairs, PAIR, keys), BF16),
            pltpu.VMEM((pairs, keys, 2 * PAIR), BF16),
        ],
        out_shape=out_shape,
        compiler_params=pltpu.CompilerParams(vmem_limit_bytes=CROSS_LIMIT),
        cost_estimate=pl.CostEstimate(
            flops=flops, bytes_accessed=12 * 2**20, transcendentals=2 * count * keys * pairs
        ),
        name="cross_first" if first else "cross_last" if last else "cross_middle",
    )(*operands)


def cross_out_kernel(core_ref, mine_ref, other_ref, x_ref, w_ref, cross_ref, norm_ref):
    pairs = mine_ref.shape[0]
    half = pairs * PAIR
    made = None
    for ref, core in ((mine_ref, core_ref[0]), (other_ref, 1 - core_ref[0])):
        rows = jnp.concatenate([ref[pair] for pair in range(pairs)], axis=-1)
        part = dot(rows, w_ref[pl.ds(pl.multiple_of(core * half, half), half), :])
        made = part if made is None else made + part
    cross_ref[...] = made.astype(BF16)
    residual = x_ref[...].astype(F32) + cross_ref[...].astype(F32)
    norm_ref[...] = layer_norm(residual)


def cross_out(core, mine, other, tokens, w_cross_out):
    rows, features = tokens.shape
    return pl.pallas_call(
        cross_out_kernel,
        in_specs=[SMEM_SPEC] + [VMEM_SPEC] * 4,
        out_specs=[VMEM_SPEC] * 2,
        out_shape=[jax.ShapeDtypeStruct((rows, features), BF16)] * 2,
        compiler_params=pltpu.CompilerParams(vmem_limit_bytes=CROSS_LIMIT),
        cost_estimate=pl.CostEstimate(
            flops=2 * rows * features * features, bytes_accessed=6 * 2**20, transcendentals=0
        ),
        name="cross_out",
    )(core, mine, other, tokens, w_cross_out)


GROUP = 16
BLOCKS = 16


def temporal_kernel(place_ref, x_ref, *refs):
    w_refs, (out_ref, x_s, att_s) = refs[:2], refs[2:]
    frames, positions, features = x_ref.shape
    groups = positions // GROUP
    size = frames * GROUP
    half = features // 2
    heads = QUAD // HD
    core, own_half = place_ref[0], place_ref[1]

    for group in range(groups):
        for frame in range(frames):
            start = group * size + frame * GROUP
            x_s[start : start + GROUP, :] = x_ref[frame, group * GROUP : (group + 1) * GROUP, :]

    def halves(ref):
        return [
            ref[:, pl.ds(pl.multiple_of(which * half, half), half)]
            for which in (own_half, 1 - own_half)
        ]

    def part_of(ref, side, columns):
        block = ref.shape[0] // BLOCKS
        starts = range(side * block, ref.shape[0], 2 * block)
        return jnp.concatenate([ref[start : start + block, columns] for start in starts], axis=0)

    def times(value_s, ref, columns):
        own, other = halves(value_s)
        return dot(own, part_of(ref, 0, columns)) + dot(other, part_of(ref, 1, columns))

    row = lax.broadcasted_iota(jnp.int32, (heads * size, size), 0)
    column = lax.broadcasted_iota(jnp.int32, (heads * size, size), 1)
    same = row % GROUP == column % GROUP
    head_of = lax.broadcasted_iota(jnp.int32, (size, QUAD), 1) // HD
    for side in range(2):
        for quad in range(half // QUAD):

            def project(which):
                columns = slice(which * half + quad * QUAD, which * half + (quad + 1) * QUAD)
                return times(x_s, w_refs[side], columns)

            queries = (project(0) * (HD**-0.5 * LOG2E)).astype(BF16)
            keys = project(1).astype(BF16)
            values = project(2).astype(BF16)
            which_core = core if side == 0 else 1 - core
            place = pl.multiple_of(which_core * half + quad * QUAD, QUAD)
            for group in range(groups):
                part = slice(group * size, (group + 1) * size)
                stacked = jnp.concatenate(
                    [queries[part] * lanes_of(QUAD, head) for head in range(heads)], axis=0
                )
                scores = jnp.where(same, dot(stacked, keys[part].T), -jnp.inf)
                weights = jnp.exp2(scores - jnp.max(scores, axis=-1, keepdims=True))
                total = jnp.sum(weights, axis=-1, keepdims=True)
                result = dot(weights.astype(BF16), values[part]) / total
                attended = result[:size]
                for head in range(1, heads):
                    attended = jnp.where(
                        head_of == head, result[head * size : (head + 1) * size], attended
                    )
                att_s[part, pl.ds(place, QUAD)] = attended.astype(BF16)

    for side in range(2):
        made = times(att_s, w_refs[side], slice(3 * half, 4 * half))
        place = pl.ds(pl.multiple_of((core if side == 0 else 1 - core) * half, half), half)
        made = made.astype(BF16)
        for group in range(groups):
            for frame in range(frames):
                start = group * size + frame * GROUP
                out_ref[frame, group * GROUP : (group + 1) * GROUP, place] = made[
                    start : start + GROUP
                ]


def temporal(place, rows, weights):
    frames, positions, features = rows.shape
    count = frames * positions
    return pl.pallas_call(
        temporal_kernel,
        in_specs=[SMEM_SPEC] + [VMEM_SPEC] * 3,
        out_specs=VMEM_SPEC,
        scratch_shapes=[pltpu.VMEM((count, features), BF16)] * 2,
        out_shape=jax.ShapeDtypeStruct(rows.shape, BF16),
        compiler_params=pltpu.CompilerParams(vmem_limit_bytes=CROSS_LIMIT),
        cost_estimate=pl.CostEstimate(
            flops=8 * count * features * features, bytes_accessed=10 * 2**20, transcendentals=0
        ),
        name="temporal",
    )(place, rows, *weights)


VIEW = ("xl", "z")
FRAME = ("y", "xh")
SWAP = [(0, 1), (1, 0)]


def across(value):
    pairs = []
    for xl in range(2):
        for xh in range(2):
            for core in range(2):
                target = (1 - xl) * 4 + (xh ^ core) * 2 + core
                pairs.append((xl * 4 + xh * 2 + core, target))
    return lax.ppermute(value, ("xl", "xh", "c"), pairs)


def per_device(tokens, w_cross_qkv, w_cross_out, w_temporal_qkv, w_temporal_out):
    own = tokens[0]
    rows, features = own.shape
    half = features // 2
    core_index = lax.axis_index("c")
    core = core_index.astype(jnp.int32).reshape(1)
    place = jnp.stack([core_index, lax.axis_index("xl")]).astype(jnp.int32)
    views = lax.axis_size(VIEW)
    forward = [(i, (i + 1) % views) for i in range(views)]
    backward = [(i, (i - 1) % views) for i in range(views)]

    swap = lambda value: lax.ppermute(value, "c", SWAP)
    partner = swap(own)
    cut = rows * 2 // 3
    chunks = [own[:cut], own[cut:]]
    around = [
        [lax.ppermute(chunk, VIEW, pairs) for pairs in (forward, backward)] for chunk in chunks
    ]

    sides = [
        jnp.concatenate(
            [
                w[:, start + side * half : start + (side + 1) * half]
                for w, start in (
                    (w_temporal_qkv, 0),
                    (w_temporal_qkv, features),
                    (w_temporal_qkv, 2 * features),
                    (w_temporal_out, 0),
                )
            ],
            axis=1,
        )
        for side in range(2)
    ]
    shard = jnp.where(core_index == 0, sides[0], sides[1])
    shards, own = lax.optimization_barrier((jnp.concatenate([shard, across(shard)], axis=0), own))
    gathered = lax.all_gather(shards, "z", axis=0, tiled=True)

    w_query, w_key, w_value = (
        lax.dynamic_slice_in_dim(w_cross_qkv, which * features + core_index * half, half, 1)
        for which in range(3)
    )
    state = list(cross_step((own, partner), (w_key, w_value, w_query)))
    for number, arrived in enumerate(around):
        *arrived, state[1] = lax.optimization_barrier((*arrived, state[1]))
        arrived = arrived + [swap(chunk) for chunk in arrived]
        last = number == len(around) - 1
        made = cross_step(arrived, (w_key, w_value), state, last=last)
        state = made if last else [state[0]] + list(made)
    mine, theirs = state
    other = swap(theirs)
    cross_rows, normed = cross_out(core, mine, other, own, w_cross_out)

    gathered, cross_rows = lax.optimization_barrier((gathered, cross_rows))
    frames = lax.axis_size(FRAME)
    spread = lax.all_to_all(normed, FRAME, split_axis=0, concat_axis=0, tiled=True)
    updated = temporal(
        place,
        spread.reshape(frames, rows // frames, features),
        (gathered, swap(gathered)),
    )
    temporal_rows = lax.all_to_all(
        updated.reshape(rows, features), FRAME, split_axis=0, concat_axis=0, tiled=True
    )
    return (cross_rows[None], temporal_rows[None])


def solution(mesh):
    fine = Mesh(mesh.devices.reshape(2, 8, 4, 2, 2), ("xl", "z", "y", "xh", "c"))
    by_token = P(VIEW, FRAME + ("c",), None)
    placed = (by_token, P(), P(), P(VIEW, None), P(VIEW, None))
    return jax.shard_map(
        per_device,
        mesh=fine,
        in_specs=placed,
        out_specs=(by_token, by_token),
        check_vma=False,
    )
```

```python
import functools

import jax
import jax.numpy as jnp
from jax import lax
from jax.experimental import pallas as pl
from jax.experimental.pallas import tpu as pltpu
from jax.sharding import Mesh
from jax.sharding import PartitionSpec as P

HEADS = 16
HD = 64
PAIR = 2 * HD
QUAD = 4 * HD
LOG2E = 1.4426950408889634
CROSS_LIMIT = 24 * 1024 * 1024
UNROLL = 4
F32 = jnp.float32
BF16 = jnp.bfloat16


def dot(a, b):
    return jnp.dot(a, b, preferred_element_type=F32)


def layer_norm(rows):
    centred = rows - jnp.mean(rows, axis=-1, keepdims=True)
    variance = jnp.mean(centred * centred, axis=-1, keepdims=True)
    return (centred * lax.rsqrt(variance + 1e-06)).astype(BF16)


def lanes_of(width, index, rows=1):
    lane = lax.broadcasted_iota(jnp.int32, (rows, width), 1)
    return jnp.where(lane // HD == index, 1.0, 0.0).astype(BF16)


def project_blocks(x_refs, w_refs, norm_s, q_ref, kt_s, v_s):
    pairs, _, keys = kt_s.shape
    start = 0
    for x_ref in x_refs:
        norm_s[start : start + x_ref.shape[0], :] = layer_norm(x_ref[...].astype(F32))
        start += x_ref.shape[0]

    def project(which, quad):
        return dot(norm_s[...], w_refs[which][:, quad * QUAD : (quad + 1) * QUAD])

    for quad in range(pairs // 2):
        if q_ref is not None:
            made = (project(2, quad) * (HD**-0.5 * LOG2E)).astype(BF16)
            for part in range(2):
                q_ref[2 * quad + part] = made[:, part * PAIR : (part + 1) * PAIR]
        made = project(0, quad).astype(BF16)
        for part in range(2):
            kt_s[2 * quad + part] = made[:, part * PAIR : (part + 1) * PAIR].T
        made = project(1, quad).astype(BF16)
        for part in range(2):
            v_s[2 * quad + part, :, :PAIR] = made[:, part * PAIR : (part + 1) * PAIR]
            v_s[2 * quad + part, :, PAIR:] = jnp.ones((keys, PAIR), BF16)


def attend_pairs(q_ref, kt_s, v_s, state, outs, row_block, part=None):
    pairs, count = q_ref.shape[:2]
    begin, end = (0, count) if part is None else (part * count // 2, (part + 1) * count // 2)
    low = lax.broadcasted_iota(jnp.int32, (row_block, PAIR), 1) < HD

    def attend(pair, carry):
        transposed, values = kt_s[pair], v_s[pair]
        for start in range(begin, end, row_block):
            rows = slice(start, start + row_block)
            queries = q_ref[pair, rows, :]
            peaks, sums = [], []
            for head in range(2):
                scores = dot(queries * lanes_of(PAIR, head), transposed)
                peak = jnp.max(scores, axis=-1, keepdims=True)
                weights = jnp.exp2(scores - peak).astype(BF16)
                peaks.append(peak)
                sums.append(dot(weights, values))
            peak = jnp.where(low, peaks[0], peaks[1])
            result = jnp.where(low, sums[0][:, :PAIR], sums[1][:, :PAIR])
            total = jnp.where(low, sums[0][:, PAIR:], sums[1][:, PAIR:])
            if state is not None:
                o_in, m_in, l_in = state
                highest = jnp.maximum(peak, m_in[pair, rows, :])
                old, new = jnp.exp2(m_in[pair, rows, :] - highest), jnp.exp2(peak - highest)
                result = new * result + old * o_in[pair, rows, :]
                total = new * total + old * l_in[pair, rows, :]
                peak = highest
            if part is not None:
                offset = start - begin
                outs[0][pair, offset : offset + row_block, :] = (result / total).astype(BF16)
            else:
                for out, value in zip(outs, (result, peak, total)):
                    out[pair, rows, :] = value
        return carry

    lax.fori_loop(0, pairs, attend, 0, unroll=UNROLL)


def project_kernel(x0_ref, x1_ref, wk_ref, wv_ref, wq_ref, q_ref, kt_ref, v_ref, norm_s):
    project_blocks((x0_ref, x1_ref), (wk_ref, wv_ref, wq_ref), norm_s, q_ref, kt_ref, v_ref)


def attend_kernel(row_block, q_ref, kt_ref, v_ref, *outs):
    attend_pairs(q_ref, kt_ref, v_ref, None, outs, row_block)


def project_more_kernel(blocks, *refs):
    x_refs, w_refs, (kt_ref, v_ref, norm_s) = refs[:blocks], refs[blocks:-3], refs[-3:]
    project_blocks(x_refs, w_refs, norm_s, None, kt_ref, v_ref)


def finish_kernel(row_block, part, q_ref, kt_ref, v_ref, o_ref, m_ref, l_ref, out_ref):
    attend_pairs(q_ref, kt_ref, v_ref, (o_ref, m_ref, l_ref), (out_ref,), row_block, part)


VMEM_SPEC = pl.BlockSpec(memory_space=pltpu.VMEM)
SMEM_SPEC = pl.BlockSpec(memory_space=pltpu.SMEM)


def local_kernel(kernel, name, operands, out_shape, scratch_shapes=(), scalars=0):
    return pl.pallas_call(
        kernel,
        in_specs=[SMEM_SPEC] * scalars + [VMEM_SPEC] * (len(operands) - scalars),
        out_specs=[VMEM_SPEC] * len(out_shape),
        scratch_shapes=list(scratch_shapes),
        out_shape=out_shape,
        compiler_params=pltpu.CompilerParams(vmem_limit_bytes=CROSS_LIMIT),
        cost_estimate=pl.CostEstimate(flops=10**6, bytes_accessed=10**5, transcendentals=0),
        name=name,
    )(*operands)


def cross_project(xs, weights):
    features, columns = weights[0].shape
    keys = sum(x.shape[0] for x in xs)
    pairs = columns // PAIR
    shapes = ((pairs, keys, PAIR), (pairs, PAIR, keys), (pairs, keys, 2 * PAIR))
    first = len(weights) == 3
    out_shape = [jax.ShapeDtypeStruct(shape, BF16) for shape in shapes[0 if first else 1 :]]
    scratch = [pltpu.VMEM((keys, features), BF16)]
    kernel = project_kernel if first else functools.partial(project_more_kernel, len(xs))
    name = "cross_project" if first else "cross_project_more"
    return local_kernel(kernel, name, (*xs, *weights), out_shape, scratch)


def cross_attend(queries, projected, state=None, part=None, row_block=384):
    pairs, count, width = queries.shape
    operands = (queries, *projected)
    if state is None:
        kept = [jax.ShapeDtypeStruct(queries.shape, F32)] * 3
        kernel = functools.partial(attend_kernel, row_block)
        return local_kernel(kernel, "cross_attend", operands, kept)
    out_shape = [jax.ShapeDtypeStruct((pairs, count // 2, width), BF16)]
    kernel = functools.partial(finish_kernel, row_block, part)
    return local_kernel(kernel, "cross_finish", (*operands, *state), out_shape)[0]


def cross_out_kernel(core_ref, mine_ref, other_ref, x_ref, w_ref, cross_ref, norm_ref):
    pairs = mine_ref.shape[0]
    half = pairs * PAIR
    made = None
    for ref, core in ((mine_ref, core_ref[0]), (other_ref, 1 - core_ref[0])):
        rows = jnp.concatenate([ref[pair] for pair in range(pairs)], axis=-1)
        part = dot(rows, w_ref[pl.ds(pl.multiple_of(core * half, half), half), :])
        made = part if made is None else made + part
    cross_ref[...] = made.astype(BF16)
    residual = x_ref[...].astype(F32) + cross_ref[...].astype(F32)
    norm_ref[...] = layer_norm(residual)


def cross_out(core, mine, other, tokens, w_cross_out):
    out_shape = [jax.ShapeDtypeStruct(tokens.shape, BF16)] * 2
    operands = (core, mine, other, tokens, w_cross_out)
    return local_kernel(cross_out_kernel, "cross_out", operands, out_shape, scalars=1)


GROUP = 16
BLOCKS = 16


def halves(ref, own_half):
    half = ref.shape[1] // 2
    return [
        ref[:, pl.ds(pl.multiple_of(which * half, half), half)]
        for which in (own_half, 1 - own_half)
    ]


def times(ref, w_ref, columns, own_half):
    block = w_ref.shape[0] // BLOCKS
    made = None
    for side, rows in enumerate(halves(ref, own_half)):
        starts = range(side * block, w_ref.shape[0], 2 * block)
        part = jnp.concatenate([w_ref[start : start + block, columns] for start in starts], axis=0)
        made = dot(rows, part) if made is None else made + dot(rows, part)
    return made


def grouped(shape):
    frames, positions, _ = shape
    for group in range(positions // GROUP):
        for frame in range(frames):
            start = (group * frames + frame) * GROUP
            yield slice(start, start + GROUP), frame, slice(group * GROUP, (group + 1) * GROUP)


def temporal_heads(x_ref, w_ref, own_half, x_s, store):
    frames, positions, features = x_ref.shape
    size = frames * GROUP
    half = features // 2
    heads = QUAD // HD
    for rows, frame, place in grouped(x_ref.shape):
        x_s[rows, :] = x_ref[frame, place, :]
    row = lax.broadcasted_iota(jnp.int32, (heads * size, size), 0)
    column = lax.broadcasted_iota(jnp.int32, (heads * size, size), 1)
    same = row % GROUP == column % GROUP
    head_of = lax.broadcasted_iota(jnp.int32, (size, QUAD), 1) // HD
    for quad in range(half // QUAD):

        def project(which):
            start = which * half + quad * QUAD
            return times(x_s, w_ref, slice(start, start + QUAD), own_half)

        queries = (project(0) * (HD**-0.5 * LOG2E)).astype(BF16)
        keys = project(1).astype(BF16)
        values = project(2).astype(BF16)
        for group in range(positions // GROUP):
            part = slice(group * size, (group + 1) * size)
            stacked = jnp.concatenate(
                [queries[part] * lanes_of(QUAD, head) for head in range(heads)], axis=0
            )
            scores = jnp.where(same, dot(stacked, keys[part].T), -jnp.inf)
            weights = jnp.exp2(scores - jnp.max(scores, axis=-1, keepdims=True))
            total = jnp.sum(weights, axis=-1, keepdims=True)
            result = dot(weights.astype(BF16), values[part]) / total
            attended = result[:size]
            for head in range(1, heads):
                attended = jnp.where(
                    head_of == head, result[head * size : (head + 1) * size], attended
                )
            store(part, quad * QUAD, attended.astype(BF16))


def temporal_mine_kernel(place_ref, x_ref, w_ref, att_ref, x_s):
    def store(rows, start, value):
        att_ref[rows, start : start + QUAD] = value

    temporal_heads(x_ref, w_ref, place_ref[1], x_s, store)


def temporal_other_kernel(place_ref, x_ref, wm_ref, wo_ref, att_ref, out_ref, x_s, att_s):
    features = x_ref.shape[2]
    half = features // 2
    core, own_half = place_ref[0], place_ref[1]
    mine, other = pl.multiple_of(core * half, half), pl.multiple_of((1 - core) * half, half)
    att_s[:, pl.ds(mine, half)] = att_ref[...]

    def store(rows, start, value):
        att_s[rows, pl.ds(pl.multiple_of(other + start, QUAD), QUAD)] = value

    temporal_heads(x_ref, wo_ref, own_half, x_s, store)
    for start, w_ref in ((mine, wm_ref), (other, wo_ref)):
        made = times(att_s, w_ref, slice(3 * half, 4 * half), own_half).astype(BF16)
        for rows, frame, place in grouped(x_ref.shape):
            out_ref[frame, place, pl.ds(start, half)] = made[rows]


def assemble_kernel(place_ref, *refs):
    blocks, out_ref = refs[:-1], refs[-1]
    size = blocks[0].shape[0]
    count = out_ref.shape[0] // size
    own = place_ref[2]

    def rows(step, start, length):
        index = lax.rem(own + step + count, count)
        return pl.ds(pl.multiple_of(index * size + start, length), length)

    for ref, step in zip(blocks, (0, -1, 1, -2, 2, -3, 3)):
        out_ref[rows(step, 0, size), :] = ref[...]
    half = size // 2
    out_ref[rows(4, 0, half), :] = blocks[7][...]
    out_ref[rows(4, half, half), :] = blocks[8][...]


def assemble(place, blocks):
    size, columns = blocks[0].shape
    out_shape = [jax.ShapeDtypeStruct((8 * size, columns), BF16)]
    return local_kernel(assemble_kernel, "assemble", (place, *blocks), out_shape, (), 1)[0]


def temporal_mine(place, rows, weights):
    frames, positions, features = rows.shape
    count = frames * positions
    out_shape = [jax.ShapeDtypeStruct((count, features // 2), BF16)]
    scratch = [pltpu.VMEM((count, features), BF16)]
    operands = (place, rows, weights)
    return local_kernel(temporal_mine_kernel, "temporal_mine", operands, out_shape, scratch, 1)[0]


def temporal_other(place, rows, mine, other, attended):
    frames, positions, features = rows.shape
    out_shape = [jax.ShapeDtypeStruct(rows.shape, BF16)]
    scratch = [pltpu.VMEM((frames * positions, features), BF16)] * 2
    operands = (place, rows, mine, other, attended)
    return local_kernel(temporal_other_kernel, "temporal_other", operands, out_shape, scratch, 1)[0]


VIEW = ("xl", "z")
FRAME = ("y", "xh")
SWAP = [(0, 1), (1, 0)]


def across(value):
    pairs = []
    for xl in range(2):
        for xh in range(2):
            for core in range(2):
                target = (1 - xl) * 4 + (xh ^ core) * 2 + core
                pairs.append((xl * 4 + xh * 2 + core, target))
    return lax.ppermute(value, ("xl", "xh", "c"), pairs)


def along(value, steps):
    return lax.ppermute(value, "z", [(i, (i + steps) % 8) for i in range(8)])


def per_device(tokens, w_cross_qkv, w_cross_out, w_temporal_qkv, w_temporal_out):
    own = tokens[0]
    rows, features = own.shape
    half = features // 2
    core_index = lax.axis_index("c")
    core = core_index.astype(jnp.int32).reshape(1)
    place = jnp.stack([core_index, lax.axis_index("xl"), lax.axis_index("z")]).astype(jnp.int32)
    views = lax.axis_size(VIEW)
    forward = [(i, (i + 1) % views) for i in range(views)]
    backward = [(i, (i - 1) % views) for i in range(views)]

    swap = lambda value: lax.ppermute(value, "c", SWAP)
    partner = swap(own)
    before, after = (lax.ppermute(own, VIEW, pairs) for pairs in (forward, backward))

    sides = [
        jnp.concatenate(
            [
                w[:, start + side * half : start + (side + 1) * half]
                for w, start in (
                    (w_temporal_qkv, 0),
                    (w_temporal_qkv, features),
                    (w_temporal_qkv, 2 * features),
                    (w_temporal_out, 0),
                )
            ],
            axis=1,
        )
        for side in range(2)
    ]
    shard = jnp.where(core_index == 0, sides[0], sides[1])
    w_query, w_key, w_value = (
        lax.dynamic_slice_in_dim(w_cross_qkv, which * features + core_index * half, half, 1)
        for which in range(3)
    )
    weights = (w_key, w_value)
    queries, *projected = cross_project((own, partner), (*weights, w_query))
    shard, queries = lax.optimization_barrier((shard, queries))
    blocks = [jnp.concatenate([shard, across(shard)], axis=0)]
    blocks += [along(blocks[0], 1), along(blocks[0], -1)]
    state = list(cross_attend(queries, projected))
    before, after, state[0] = lax.optimization_barrier((before, after, state[0]))
    arrived = (before, after, swap(before), swap(after))
    projected = cross_project(arrived, weights)
    theirs = cross_attend(queries, projected, state, part=1)
    blocks[1], blocks[2], theirs = lax.optimization_barrier((blocks[1], blocks[2], theirs))
    blocks += [along(blocks[1], 1), along(blocks[2], -1)]
    other = swap(theirs)
    mine = cross_attend(queries, projected, state, part=0)
    cross_rows, normed = cross_out(core, mine, other, own, w_cross_out)

    blocks[3], blocks[4], normed = lax.optimization_barrier((blocks[3], blocks[4], normed))
    cut = blocks[0].shape[0] // 2
    blocks += [along(blocks[3], 1), along(blocks[4], -1)]
    blocks += [along(blocks[3][:cut], 2), along(blocks[4][cut:], -2)]
    frames = lax.axis_size(FRAME)
    spread = lax.all_to_all(normed, FRAME, split_axis=0, concat_axis=0, tiled=True)
    *blocks, spread = lax.optimization_barrier((*blocks, spread))
    gathered = assemble(place, blocks)
    spread = spread.reshape(frames, rows // frames, features)
    gathered_other = swap(gathered)
    attended = temporal_mine(place, spread, gathered)
    gathered_other, attended = lax.optimization_barrier((gathered_other, attended))
    updated = temporal_other(place, spread, gathered, gathered_other, attended)
    temporal_rows = lax.all_to_all(
        updated.reshape(rows, features), FRAME, split_axis=0, concat_axis=0, tiled=True
    )
    return (cross_rows[None], temporal_rows[None])


def solution(mesh):
    fine = Mesh(mesh.devices.reshape(2, 8, 4, 2, 2), ("xl", "z", "y", "xh", "c"))
    by_token = P(VIEW, FRAME + ("c",), None)
    placed = (by_token, P(), P(), P(VIEW, None), P(VIEW, None))
    return jax.shard_map(
        per_device,
        mesh=fine,
        in_specs=placed,
        out_specs=(by_token, by_token),
        check_vma=False,
    )
```

```python
import functools

import jax
import jax.numpy as jnp
from jax import lax
from jax.experimental import pallas as pl
from jax.experimental.pallas import tpu as pltpu
from jax.sharding import Mesh
from jax.sharding import PartitionSpec as P

HEADS = 16
HD = 64
PAIR = 2 * HD
QUAD = 4 * HD
LOG2E = 1.4426950408889634
CROSS_LIMIT = 24 * 1024 * 1024
UNROLL = 4
F32 = jnp.float32
BF16 = jnp.bfloat16


def dot(a, b):
    return jnp.dot(a, b, preferred_element_type=F32)


def layer_norm(rows):
    centred = rows - jnp.mean(rows, axis=-1, keepdims=True)
    variance = jnp.mean(centred * centred, axis=-1, keepdims=True)
    return (centred * lax.rsqrt(variance + 1e-06)).astype(BF16)


def lanes_of(width, index, rows=1):
    lane = lax.broadcasted_iota(jnp.int32, (rows, width), 1)
    return jnp.where(lane // HD == index, 1.0, 0.0).astype(BF16)


def project_blocks(x_refs, w_refs, norm_s, q_ref, kt_s, v_s):
    pairs, _, keys = kt_s.shape
    start = 0
    for x_ref in x_refs:
        norm_s[start : start + x_ref.shape[0], :] = layer_norm(x_ref[...].astype(F32))
        start += x_ref.shape[0]

    def project(which, quad):
        return dot(norm_s[...], w_refs[which][:, quad * QUAD : (quad + 1) * QUAD])

    for quad in range(pairs // 2):
        if q_ref is not None:
            made = (project(2, quad) * (HD**-0.5 * LOG2E)).astype(BF16)
            for part in range(2):
                q_ref[2 * quad + part] = made[:, part * PAIR : (part + 1) * PAIR]
        made = project(0, quad).astype(BF16)
        for part in range(2):
            kt_s[2 * quad + part] = made[:, part * PAIR : (part + 1) * PAIR].T
        made = project(1, quad).astype(BF16)
        for part in range(2):
            v_s[2 * quad + part, :, :PAIR] = made[:, part * PAIR : (part + 1) * PAIR]
            v_s[2 * quad + part, :, PAIR:] = jnp.ones((keys, PAIR), BF16)


def attend_pairs(q_ref, kt_s, v_s, state, outs, row_block, part=None):
    pairs, count = q_ref.shape[:2]
    begin, end = (0, count) if part is None else (part * count // 2, (part + 1) * count // 2)
    low = lax.broadcasted_iota(jnp.int32, (row_block, PAIR), 1) < HD

    def attend(pair, carry):
        transposed, values = kt_s[pair], v_s[pair]
        for start in range(begin, end, row_block):
            rows = slice(start, start + row_block)
            queries = q_ref[pair, rows, :]
            peaks, sums = [], []
            for head in range(2):
                scores = dot(queries * lanes_of(PAIR, head), transposed)
                peak = jnp.max(scores, axis=-1, keepdims=True)
                weights = jnp.exp2(scores - peak).astype(BF16)
                peaks.append(peak)
                sums.append(dot(weights, values))
            peak = jnp.where(low, peaks[0], peaks[1])
            result = jnp.where(low, sums[0][:, :PAIR], sums[1][:, :PAIR])
            total = jnp.where(low, sums[0][:, PAIR:], sums[1][:, PAIR:])
            if state is not None:
                o_in, m_in, l_in = state
                highest = jnp.maximum(peak, m_in[pair, rows, :])
                old, new = jnp.exp2(m_in[pair, rows, :] - highest), jnp.exp2(peak - highest)
                result = new * result + old * o_in[pair, rows, :]
                total = new * total + old * l_in[pair, rows, :]
                peak = highest
            if part is not None:
                offset = start - begin
                outs[0][pair, offset : offset + row_block, :] = (result / total).astype(BF16)
            else:
                for out, value in zip(outs, (result, peak, total)):
                    out[pair, rows, :] = value
        return carry

    lax.fori_loop(0, pairs, attend, 0, unroll=UNROLL)


def project_kernel(x0_ref, x1_ref, wk_ref, wv_ref, wq_ref, q_ref, kt_ref, v_ref, norm_s):
    project_blocks((x0_ref, x1_ref), (wk_ref, wv_ref, wq_ref), norm_s, q_ref, kt_ref, v_ref)


def attend_kernel(row_block, q_ref, kt_ref, v_ref, *outs):
    attend_pairs(q_ref, kt_ref, v_ref, None, outs, row_block)


def project_more_kernel(blocks, *refs):
    x_refs, w_refs, (kt_ref, v_ref, norm_s) = refs[:blocks], refs[blocks:-3], refs[-3:]
    project_blocks(x_refs, w_refs, norm_s, None, kt_ref, v_ref)


def finish_kernel(row_block, part, q_ref, kt_ref, v_ref, o_ref, m_ref, l_ref, out_ref):
    attend_pairs(q_ref, kt_ref, v_ref, (o_ref, m_ref, l_ref), (out_ref,), row_block, part)


VMEM_SPEC = pl.BlockSpec(memory_space=pltpu.VMEM)
SMEM_SPEC = pl.BlockSpec(memory_space=pltpu.SMEM)


def local_kernel(kernel, name, operands, out_shape, scratch_shapes=(), scalars=0):
    return pl.pallas_call(
        kernel,
        in_specs=[SMEM_SPEC] * scalars + [VMEM_SPEC] * (len(operands) - scalars),
        out_specs=[VMEM_SPEC] * len(out_shape),
        scratch_shapes=list(scratch_shapes),
        out_shape=out_shape,
        compiler_params=pltpu.CompilerParams(vmem_limit_bytes=CROSS_LIMIT),
        cost_estimate=pl.CostEstimate(flops=10**6, bytes_accessed=10**5, transcendentals=0),
        name=name,
    )(*operands)


def cross_project(xs, weights):
    features, columns = weights[0].shape
    keys = sum(x.shape[0] for x in xs)
    pairs = columns // PAIR
    shapes = ((pairs, keys, PAIR), (pairs, PAIR, keys), (pairs, keys, 2 * PAIR))
    first = len(weights) == 3
    out_shape = [jax.ShapeDtypeStruct(shape, BF16) for shape in shapes[0 if first else 1 :]]
    scratch = [pltpu.VMEM((keys, features), BF16)]
    kernel = project_kernel if first else functools.partial(project_more_kernel, len(xs))
    name = "cross_project" if first else "cross_project_more"
    return local_kernel(kernel, name, (*xs, *weights), out_shape, scratch)


def cross_attend(queries, projected, state=None, part=None, row_block=384):
    pairs, count, width = queries.shape
    operands = (queries, *projected)
    if state is None:
        kept = [jax.ShapeDtypeStruct(queries.shape, F32)] * 3
        kernel = functools.partial(attend_kernel, row_block)
        return local_kernel(kernel, "cross_attend", operands, kept)
    out_shape = [jax.ShapeDtypeStruct((pairs, count // 2, width), BF16)]
    kernel = functools.partial(finish_kernel, row_block, part)
    return local_kernel(kernel, "cross_finish", (*operands, *state), out_shape)[0]


def cross_out_kernel(core_ref, mine_ref, other_ref, x_ref, w_ref, cross_ref, norm_ref):
    pairs = mine_ref.shape[0]
    half = pairs * PAIR
    made = None
    for ref, core in ((mine_ref, core_ref[0]), (other_ref, 1 - core_ref[0])):
        rows = jnp.concatenate([ref[pair] for pair in range(pairs)], axis=-1)
        part = dot(rows, w_ref[pl.ds(pl.multiple_of(core * half, half), half), :])
        made = part if made is None else made + part
    cross_ref[...] = made.astype(BF16)
    residual = x_ref[...].astype(F32) + cross_ref[...].astype(F32)
    norm_ref[...] = layer_norm(residual)


def cross_out(core, mine, other, tokens, w_cross_out):
    out_shape = [jax.ShapeDtypeStruct(tokens.shape, BF16)] * 2
    operands = (core, mine, other, tokens, w_cross_out)
    return local_kernel(cross_out_kernel, "cross_out", operands, out_shape, scalars=1)


GROUP = 16
BLOCKS = 16


def halves(ref, own_half):
    half = ref.shape[1] // 2
    return [
        ref[:, pl.ds(pl.multiple_of(which * half, half), half)]
        for which in (own_half, 1 - own_half)
    ]


def times(ref, w_ref, columns, own_half):
    block = w_ref.shape[0] // BLOCKS
    made = None
    for side, rows in enumerate(halves(ref, own_half)):
        starts = range(side * block, w_ref.shape[0], 2 * block)
        part = jnp.concatenate([w_ref[start : start + block, columns] for start in starts], axis=0)
        made = dot(rows, part) if made is None else made + dot(rows, part)
    return made


def grouped(shape):
    frames, positions, _ = shape
    for group in range(positions // GROUP):
        for frame in range(frames):
            start = (group * frames + frame) * GROUP
            yield slice(start, start + GROUP), frame, slice(group * GROUP, (group + 1) * GROUP)


def temporal_heads(x_ref, w_ref, own_half, x_s, store):
    frames, positions, features = x_ref.shape
    size = frames * GROUP
    half = features // 2
    heads = QUAD // HD
    for rows, frame, place in grouped(x_ref.shape):
        x_s[rows, :] = x_ref[frame, place, :]
    row = lax.broadcasted_iota(jnp.int32, (heads * size, size), 0)
    column = lax.broadcasted_iota(jnp.int32, (heads * size, size), 1)
    same = row % GROUP == column % GROUP
    head_of = lax.broadcasted_iota(jnp.int32, (size, QUAD), 1) // HD
    for quad in range(half // QUAD):

        def project(which):
            start = which * half + quad * QUAD
            return times(x_s, w_ref, slice(start, start + QUAD), own_half)

        queries = (project(0) * (HD**-0.5 * LOG2E)).astype(BF16)
        keys = project(1).astype(BF16)
        values = project(2).astype(BF16)
        for group in range(positions // GROUP):
            part = slice(group * size, (group + 1) * size)
            stacked = jnp.concatenate(
                [queries[part] * lanes_of(QUAD, head) for head in range(heads)], axis=0
            )
            scores = jnp.where(same, dot(stacked, keys[part].T), -jnp.inf)
            weights = jnp.exp2(scores - jnp.max(scores, axis=-1, keepdims=True))
            total = jnp.sum(weights, axis=-1, keepdims=True)
            result = dot(weights.astype(BF16), values[part]) / total
            attended = result[:size]
            for head in range(1, heads):
                attended = jnp.where(
                    head_of == head, result[head * size : (head + 1) * size], attended
                )
            store(part, quad * QUAD, attended.astype(BF16))


def temporal_mine_kernel(place_ref, x_ref, w_ref, att_ref, x_s):
    def store(rows, start, value):
        att_ref[rows, start : start + QUAD] = value

    temporal_heads(x_ref, w_ref, place_ref[1], x_s, store)


def temporal_other_kernel(place_ref, x_ref, wm_ref, wo_ref, att_ref, out_ref, x_s, att_s):
    features = x_ref.shape[2]
    half = features // 2
    core, own_half = place_ref[0], place_ref[1]
    mine, other = pl.multiple_of(core * half, half), pl.multiple_of((1 - core) * half, half)
    att_s[:, pl.ds(mine, half)] = att_ref[...]

    def store(rows, start, value):
        att_s[rows, pl.ds(pl.multiple_of(other + start, QUAD), QUAD)] = value

    temporal_heads(x_ref, wo_ref, own_half, x_s, store)
    for start, w_ref in ((mine, wm_ref), (other, wo_ref)):
        made = times(att_s, w_ref, slice(3 * half, 4 * half), own_half).astype(BF16)
        for rows, frame, place in grouped(x_ref.shape):
            out_ref[frame, place, pl.ds(start, half)] = made[rows]


def assemble_kernel(place_ref, *refs):
    blocks, out_ref = refs[:-1], refs[-1]
    size = blocks[0].shape[0]
    count = out_ref.shape[0] // size
    own = place_ref[2]

    def rows(step, start, length):
        index = lax.rem(own + step + count, count)
        return pl.ds(pl.multiple_of(index * size + start, length), length)

    for ref, step in zip(blocks, (0, -1, 1, -2, 2, -3, 3, 4)):
        out_ref[rows(step, 0, size), :] = ref[...]


def assemble(place, blocks):
    size, columns = blocks[0].shape
    out_shape = [jax.ShapeDtypeStruct((8 * size, columns), BF16)]
    return local_kernel(assemble_kernel, "assemble", (place, *blocks), out_shape, (), 1)[0]


def temporal_mine(place, rows, weights):
    frames, positions, features = rows.shape
    count = frames * positions
    out_shape = [jax.ShapeDtypeStruct((count, features // 2), BF16)]
    scratch = [pltpu.VMEM((count, features), BF16)]
    operands = (place, rows, weights)
    return local_kernel(temporal_mine_kernel, "temporal_mine", operands, out_shape, scratch, 1)[0]


def temporal_other(place, rows, mine, other, attended):
    frames, positions, features = rows.shape
    out_shape = [jax.ShapeDtypeStruct(rows.shape, BF16)]
    scratch = [pltpu.VMEM((frames * positions, features), BF16)] * 2
    operands = (place, rows, mine, other, attended)
    return local_kernel(temporal_other_kernel, "temporal_other", operands, out_shape, scratch, 1)[0]


VIEW = ("xl", "z")
FRAME = ("y", "xh")
SWAP = [(0, 1), (1, 0)]


def across(value):
    pairs = []
    for xl in range(2):
        for xh in range(2):
            for core in range(2):
                target = (1 - xl) * 4 + (xh ^ core) * 2 + core
                pairs.append((xl * 4 + xh * 2 + core, target))
    return lax.ppermute(value, ("xl", "xh", "c"), pairs)


def along(value, steps):
    return lax.ppermute(value, "z", [(i, (i + steps) % 8) for i in range(8)])


def opposite(ahead, behind):
    value = jnp.where(lax.axis_index("c") == 0, ahead, behind)
    pairs = []
    for z in range(8):
        pairs += [(2 * z, (z + 1) % 8 * 2), (2 * z + 1, (z - 1) % 8 * 2 + 1)]
    return lax.ppermute(value, ("z", "c"), pairs)


def per_device(tokens, w_cross_qkv, w_cross_out, w_temporal_qkv, w_temporal_out):
    own = tokens[0]
    rows, features = own.shape
    half = features // 2
    core_index = lax.axis_index("c")
    core = core_index.astype(jnp.int32).reshape(1)
    place = jnp.stack([core_index, lax.axis_index("xl"), lax.axis_index("z")]).astype(jnp.int32)
    views = lax.axis_size(VIEW)
    forward = [(i, (i + 1) % views) for i in range(views)]
    backward = [(i, (i - 1) % views) for i in range(views)]

    swap = lambda value: lax.ppermute(value, "c", SWAP)
    partner = swap(own)
    before, after = (lax.ppermute(own, VIEW, pairs) for pairs in (forward, backward))

    sides = [
        jnp.concatenate(
            [
                w[:, start + side * half : start + (side + 1) * half]
                for w, start in (
                    (w_temporal_qkv, 0),
                    (w_temporal_qkv, features),
                    (w_temporal_qkv, 2 * features),
                    (w_temporal_out, 0),
                )
            ],
            axis=1,
        )
        for side in range(2)
    ]
    shard = jnp.where(core_index == 0, sides[0], sides[1])
    w_query, w_key, w_value = (
        lax.dynamic_slice_in_dim(w_cross_qkv, which * features + core_index * half, half, 1)
        for which in range(3)
    )
    weights = (w_key, w_value)
    queries, *projected = cross_project((own, partner), (*weights, w_query))
    shard, queries = lax.optimization_barrier((shard, queries))
    blocks = [jnp.concatenate([shard, across(shard)], axis=0)]
    blocks += [along(blocks[0], 1), along(blocks[0], -1)]
    state = list(cross_attend(queries, projected))
    before, after, state[0] = lax.optimization_barrier((before, after, state[0]))
    arrived = (before, after, swap(before), swap(after))
    projected = cross_project(arrived, weights)
    theirs = cross_attend(queries, projected, state, part=1)
    blocks[1], blocks[2], theirs = lax.optimization_barrier((blocks[1], blocks[2], theirs))
    blocks += [along(blocks[1], 1), along(blocks[2], -1)]
    other = swap(theirs)
    mine = cross_attend(queries, projected, state, part=0)
    *blocks, other, mine = lax.optimization_barrier((*blocks, other, mine))
    cross_rows, normed = cross_out(core, mine, other, own, w_cross_out)

    blocks += [along(blocks[3], 1), along(blocks[4], -1)]
    blocks += [opposite(blocks[5], blocks[6])]
    frames = lax.axis_size(FRAME)
    spread = lax.all_to_all(normed, FRAME, split_axis=0, concat_axis=0, tiled=True)
    *blocks, spread = lax.optimization_barrier((*blocks, spread))
    gathered = assemble(place, blocks)
    spread = spread.reshape(frames, rows // frames, features)
    gathered_other = swap(gathered)
    attended = temporal_mine(place, spread, gathered)
    gathered_other, attended = lax.optimization_barrier((gathered_other, attended))
    updated = temporal_other(place, spread, gathered, gathered_other, attended)
    temporal_rows = lax.all_to_all(
        updated.reshape(rows, features), FRAME, split_axis=0, concat_axis=0, tiled=True
    )
    return (cross_rows[None], temporal_rows[None])


def solution(mesh):
    fine = Mesh(mesh.devices.reshape(2, 8, 4, 2, 2), ("xl", "z", "y", "xh", "c"))
    by_token = P(VIEW, FRAME + ("c",), None)
    placed = (by_token, P(), P(), P(VIEW, None), P(VIEW, None))
    return jax.shard_map(
        per_device,
        mesh=fine,
        in_specs=placed,
        out_specs=(by_token, by_token),
        check_vma=False,
    )
```

```python
import functools

import jax
import jax.numpy as jnp
from jax import lax
from jax.experimental import pallas as pl
from jax.experimental.pallas import tpu as pltpu
from jax.sharding import Mesh
from jax.sharding import PartitionSpec as P

HEADS = 16
HD = 64
PAIR = 2 * HD
QUAD = 4 * HD
LOG2E = 1.4426950408889634
CROSS_LIMIT = 24 * 1024 * 1024
UNROLL = 2
F32 = jnp.float32
BF16 = jnp.bfloat16


def dot(a, b):
    return jnp.dot(a, b, preferred_element_type=F32)


def layer_norm(rows):
    centred = rows - jnp.mean(rows, axis=-1, keepdims=True)
    variance = jnp.mean(centred * centred, axis=-1, keepdims=True)
    return (centred * lax.rsqrt(variance + 1e-06)).astype(BF16)


def lanes_of(width, index, rows=1):
    lane = lax.broadcasted_iota(jnp.int32, (rows, width), 1)
    return jnp.where(lane // HD == index, 1.0, 0.0).astype(BF16)


def project_blocks(x_refs, w_refs, norm_s, q_ref, kt_s, v_s):
    pairs, _, keys = kt_s.shape
    start = 0
    for x_ref in x_refs:
        norm_s[start : start + x_ref.shape[0], :] = layer_norm(x_ref[...].astype(F32))
        start += x_ref.shape[0]

    def project(which, quad):
        return dot(norm_s[...], w_refs[which][:, quad * QUAD : (quad + 1) * QUAD])

    for quad in range(pairs // 2):
        if q_ref is not None:
            made = (project(2, quad) * (HD**-0.5 * LOG2E)).astype(BF16)
            for part in range(2):
                q_ref[2 * quad + part] = made[:, part * PAIR : (part + 1) * PAIR]
        made = project(0, quad).astype(BF16)
        for part in range(2):
            kt_s[2 * quad + part] = made[:, part * PAIR : (part + 1) * PAIR].T
        made = project(1, quad).astype(BF16)
        for part in range(2):
            v_s[2 * quad + part, :, :PAIR] = made[:, part * PAIR : (part + 1) * PAIR]
            v_s[2 * quad + part, :, PAIR:] = jnp.ones((keys, PAIR), BF16)


def attend_pairs(q_ref, kt_s, v_s, state, outs, row_block, part=None):
    pairs, count = q_ref.shape[:2]
    begin, end = (0, count) if part is None else (part * count // 2, (part + 1) * count // 2)
    low = lax.broadcasted_iota(jnp.int32, (row_block, PAIR), 1) < HD

    def attend(pair, carry):
        transposed, values = kt_s[pair], v_s[pair]
        for start in range(begin, end, row_block):
            rows = slice(start, start + row_block)
            queries = q_ref[pair, rows, :]
            peaks, sums = [], []
            for head in range(2):
                scores = dot(queries * lanes_of(PAIR, head), transposed)
                peak = jnp.max(scores, axis=-1, keepdims=True)
                weights = jnp.exp2(scores - peak).astype(BF16)
                peaks.append(peak)
                sums.append(dot(weights, values))
            peak = jnp.where(low, peaks[0], peaks[1])
            result = jnp.where(low, sums[0][:, :PAIR], sums[1][:, :PAIR])
            total = jnp.where(low, sums[0][:, PAIR:], sums[1][:, PAIR:])
            if state is not None:
                o_in, m_in, l_in = state
                highest = jnp.maximum(peak, m_in[pair, rows, :])
                old, new = jnp.exp2(m_in[pair, rows, :] - highest), jnp.exp2(peak - highest)
                result = new * result + old * o_in[pair, rows, :]
                total = new * total + old * l_in[pair, rows, :]
                peak = highest
            if part is not None:
                offset = start - begin
                outs[0][pair, offset : offset + row_block, :] = (result / total).astype(BF16)
            else:
                for out, value in zip(outs, (result, peak, total)):
                    out[pair, rows, :] = value
        return carry

    lax.fori_loop(0, pairs, attend, 0, unroll=UNROLL)


def project_kernel(x0_ref, x1_ref, wk_ref, wv_ref, wq_ref, q_ref, kt_ref, v_ref, norm_s):
    project_blocks((x0_ref, x1_ref), (wk_ref, wv_ref, wq_ref), norm_s, q_ref, kt_ref, v_ref)


def attend_kernel(row_block, q_ref, kt_ref, v_ref, *outs):
    attend_pairs(q_ref, kt_ref, v_ref, None, outs, row_block)


def project_more_kernel(blocks, *refs):
    x_refs, w_refs, (kt_ref, v_ref, norm_s) = refs[:blocks], refs[blocks:-3], refs[-3:]
    project_blocks(x_refs, w_refs, norm_s, None, kt_ref, v_ref)


def finish_kernel(row_block, part, q_ref, kt_ref, v_ref, o_ref, m_ref, l_ref, out_ref):
    attend_pairs(q_ref, kt_ref, v_ref, (o_ref, m_ref, l_ref), (out_ref,), row_block, part)


VMEM_SPEC = pl.BlockSpec(memory_space=pltpu.VMEM)
SMEM_SPEC = pl.BlockSpec(memory_space=pltpu.SMEM)


def local_kernel(kernel, name, operands, out_shape, scratch_shapes=(), scalars=0):
    return pl.pallas_call(
        kernel,
        in_specs=[SMEM_SPEC] * scalars + [VMEM_SPEC] * (len(operands) - scalars),
        out_specs=[VMEM_SPEC] * len(out_shape),
        scratch_shapes=list(scratch_shapes),
        out_shape=out_shape,
        compiler_params=pltpu.CompilerParams(vmem_limit_bytes=CROSS_LIMIT),
        cost_estimate=pl.CostEstimate(flops=10**6, bytes_accessed=10**5, transcendentals=0),
        name=name,
    )(*operands)


def cross_project(xs, weights):
    features, columns = weights[0].shape
    keys = sum(x.shape[0] for x in xs)
    pairs = columns // PAIR
    shapes = ((pairs, keys, PAIR), (pairs, PAIR, keys), (pairs, keys, 2 * PAIR))
    first = len(weights) == 3
    out_shape = [jax.ShapeDtypeStruct(shape, BF16) for shape in shapes[0 if first else 1 :]]
    scratch = [pltpu.VMEM((keys, features), BF16)]
    kernel = project_kernel if first else functools.partial(project_more_kernel, len(xs))
    name = "cross_project" if first else "cross_project_more"
    return local_kernel(kernel, name, (*xs, *weights), out_shape, scratch)


def cross_attend(queries, projected, state=None, part=None, row_block=384):
    pairs, count, width = queries.shape
    operands = (queries, *projected)
    if state is None:
        kept = [jax.ShapeDtypeStruct(queries.shape, F32)] * 3
        kernel = functools.partial(attend_kernel, row_block)
        return local_kernel(kernel, "cross_attend", operands, kept)
    out_shape = [jax.ShapeDtypeStruct((pairs, count // 2, width), BF16)]
    kernel = functools.partial(finish_kernel, row_block, part)
    return local_kernel(kernel, "cross_finish", (*operands, *state), out_shape)[0]


def cross_out_kernel(core_ref, mine_ref, other_ref, x_ref, w_ref, cross_ref, norm_ref):
    pairs = mine_ref.shape[0]
    half = pairs * PAIR
    made = None
    for ref, core in ((mine_ref, core_ref[0]), (other_ref, 1 - core_ref[0])):
        rows = jnp.concatenate([ref[pair] for pair in range(pairs)], axis=-1)
        part = dot(rows, w_ref[pl.ds(pl.multiple_of(core * half, half), half), :])
        made = part if made is None else made + part
    cross_ref[...] = made.astype(BF16)
    residual = x_ref[...].astype(F32) + cross_ref[...].astype(F32)
    norm_ref[...] = layer_norm(residual)


def cross_out(core, mine, other, tokens, w_cross_out):
    out_shape = [jax.ShapeDtypeStruct(tokens.shape, BF16)] * 2
    operands = (core, mine, other, tokens, w_cross_out)
    return local_kernel(cross_out_kernel, "cross_out", operands, out_shape, scalars=1)


GROUP = 16
BLOCKS = 16


def halves(ref, own_half):
    half = ref.shape[1] // 2
    return [
        ref[:, pl.ds(pl.multiple_of(which * half, half), half)]
        for which in (own_half, 1 - own_half)
    ]


def times(ref, w_ref, columns, own_half):
    block = w_ref.shape[0] // BLOCKS
    made = None
    for side, rows in enumerate(halves(ref, own_half)):
        starts = range(side * block, w_ref.shape[0], 2 * block)
        part = jnp.concatenate([w_ref[start : start + block, columns] for start in starts], axis=0)
        made = dot(rows, part) if made is None else made + dot(rows, part)
    return made


def grouped(shape):
    frames, positions, _ = shape
    for group in range(positions // GROUP):
        for frame in range(frames):
            start = (group * frames + frame) * GROUP
            yield slice(start, start + GROUP), frame, slice(group * GROUP, (group + 1) * GROUP)


def temporal_heads(x_ref, w_ref, own_half, x_s, store):
    frames, positions, features = x_ref.shape
    size = frames * GROUP
    half = features // 2
    heads = QUAD // HD
    for rows, frame, place in grouped(x_ref.shape):
        x_s[rows, :] = x_ref[frame, place, :]
    row = lax.broadcasted_iota(jnp.int32, (heads * size, size), 0)
    column = lax.broadcasted_iota(jnp.int32, (heads * size, size), 1)
    same = row % GROUP == column % GROUP
    head_of = lax.broadcasted_iota(jnp.int32, (size, QUAD), 1) // HD
    for quad in range(half // QUAD):

        def project(which):
            start = which * half + quad * QUAD
            return times(x_s, w_ref, slice(start, start + QUAD), own_half)

        queries = (project(0) * (HD**-0.5 * LOG2E)).astype(BF16)
        keys = project(1).astype(BF16)
        values = project(2).astype(BF16)
        for group in range(positions // GROUP):
            part = slice(group * size, (group + 1) * size)
            stacked = jnp.concatenate(
                [queries[part] * lanes_of(QUAD, head) for head in range(heads)], axis=0
            )
            scores = jnp.where(same, dot(stacked, keys[part].T), -jnp.inf)
            weights = jnp.exp2(scores - jnp.max(scores, axis=-1, keepdims=True))
            total = jnp.sum(weights, axis=-1, keepdims=True)
            result = dot(weights.astype(BF16), values[part]) / total
            attended = result[:size]
            for head in range(1, heads):
                attended = jnp.where(
                    head_of == head, result[head * size : (head + 1) * size], attended
                )
            store(part, quad * QUAD, attended.astype(BF16))


def temporal_mine_kernel(place_ref, x_ref, w_ref, att_ref, x_s):
    def store(rows, start, value):
        att_ref[rows, start : start + QUAD] = value

    temporal_heads(x_ref, w_ref, place_ref[1], x_s, store)


def temporal_other_kernel(place_ref, x_ref, wm_ref, wo_ref, att_ref, out_ref, x_s, att_s):
    features = x_ref.shape[2]
    half = features // 2
    core, own_half = place_ref[0], place_ref[1]
    mine, other = pl.multiple_of(core * half, half), pl.multiple_of((1 - core) * half, half)
    att_s[:, pl.ds(mine, half)] = att_ref[...]

    def store(rows, start, value):
        att_s[rows, pl.ds(pl.multiple_of(other + start, QUAD), QUAD)] = value

    temporal_heads(x_ref, wo_ref, own_half, x_s, store)
    for start, w_ref in ((mine, wm_ref), (other, wo_ref)):
        made = times(att_s, w_ref, slice(3 * half, 4 * half), own_half).astype(BF16)
        for rows, frame, place in grouped(x_ref.shape):
            out_ref[frame, place, pl.ds(start, half)] = made[rows]


def assemble_kernel(place_ref, *refs):
    blocks, out_ref = refs[:-1], refs[-1]
    size = blocks[0].shape[0]
    count = out_ref.shape[0] // size
    own = place_ref[2]

    def rows(step, start, length):
        index = lax.rem(own + step + count, count)
        return pl.ds(pl.multiple_of(index * size + start, length), length)

    for ref, step in zip(blocks, (0, -1, 1, -2, 2, -3, 3, 4)):
        out_ref[rows(step, 0, size), :] = ref[...]


def assemble(place, blocks):
    size, columns = blocks[0].shape
    out_shape = [jax.ShapeDtypeStruct((8 * size, columns), BF16)]
    return local_kernel(assemble_kernel, "assemble", (place, *blocks), out_shape, (), 1)[0]


def temporal_mine(place, rows, weights):
    frames, positions, features = rows.shape
    count = frames * positions
    out_shape = [jax.ShapeDtypeStruct((count, features // 2), BF16)]
    scratch = [pltpu.VMEM((count, features), BF16)]
    operands = (place, rows, weights)
    return local_kernel(temporal_mine_kernel, "temporal_mine", operands, out_shape, scratch, 1)[0]


def temporal_other(place, rows, mine, other, attended):
    frames, positions, features = rows.shape
    out_shape = [jax.ShapeDtypeStruct(rows.shape, BF16)]
    scratch = [pltpu.VMEM((frames * positions, features), BF16)] * 2
    operands = (place, rows, mine, other, attended)
    return local_kernel(temporal_other_kernel, "temporal_other", operands, out_shape, scratch, 1)[0]


VIEW = ("xl", "z")
FRAME = ("y", "xh")
SWAP = [(0, 1), (1, 0)]


def across(value):
    pairs = []
    for xl in range(2):
        for xh in range(2):
            for core in range(2):
                target = (1 - xl) * 4 + (xh ^ core) * 2 + core
                pairs.append((xl * 4 + xh * 2 + core, target))
    return lax.ppermute(value, ("xl", "xh", "c"), pairs)


def along(value, steps):
    return lax.ppermute(value, "z", [(i, (i + steps) % 8) for i in range(8)])


def opposite(ahead, behind):
    value = jnp.where(lax.axis_index("c") == 0, ahead, behind)
    pairs = []
    for z in range(8):
        pairs += [(2 * z, (z + 1) % 8 * 2), (2 * z + 1, (z - 1) % 8 * 2 + 1)]
    return lax.ppermute(value, ("z", "c"), pairs)


def per_device(tokens, w_cross_qkv, w_cross_out, w_temporal_qkv, w_temporal_out):
    own = tokens[0]
    rows, features = own.shape
    half = features // 2
    core_index = lax.axis_index("c")
    core = core_index.astype(jnp.int32).reshape(1)
    place = jnp.stack([core_index, lax.axis_index("xl"), lax.axis_index("z")]).astype(jnp.int32)
    views = lax.axis_size(VIEW)
    forward = [(i, (i + 1) % views) for i in range(views)]
    backward = [(i, (i - 1) % views) for i in range(views)]

    swap = lambda value: lax.ppermute(value, "c", SWAP)
    partner = swap(own)
    before, after = (lax.ppermute(own, VIEW, pairs) for pairs in (forward, backward))

    sides = [
        jnp.concatenate(
            [
                w[:, start + side * half : start + (side + 1) * half]
                for w, start in (
                    (w_temporal_qkv, 0),
                    (w_temporal_qkv, features),
                    (w_temporal_qkv, 2 * features),
                    (w_temporal_out, 0),
                )
            ],
            axis=1,
        )
        for side in range(2)
    ]
    shard = jnp.where(core_index == 0, sides[0], sides[1])
    w_query, w_key, w_value = (
        lax.dynamic_slice_in_dim(w_cross_qkv, which * features + core_index * half, half, 1)
        for which in range(3)
    )
    weights = (w_key, w_value)
    queries, *projected = cross_project((own, partner), (*weights, w_query))
    shard, queries = lax.optimization_barrier((shard, queries))
    blocks = [jnp.concatenate([shard, across(shard)], axis=0)]
    blocks += [along(blocks[0], 1), along(blocks[0], -1)]
    state = list(cross_attend(queries, projected))
    before, after, state[0] = lax.optimization_barrier((before, after, state[0]))
    arrived = (before, after, swap(before), swap(after))
    projected = cross_project(arrived, weights)
    theirs = cross_attend(queries, projected, state, part=1)
    blocks[1], blocks[2], theirs = lax.optimization_barrier((blocks[1], blocks[2], theirs))
    blocks += [along(blocks[1], 1), along(blocks[2], -1)]
    other = swap(theirs)
    mine = cross_attend(queries, projected, state, part=0)
    *blocks, other, mine = lax.optimization_barrier((*blocks, other, mine))
    cross_rows, normed = cross_out(core, mine, other, own, w_cross_out)

    blocks += [along(blocks[3], 1), along(blocks[4], -1)]
    blocks += [opposite(blocks[5], blocks[6])]
    frames = lax.axis_size(FRAME)
    spread = lax.all_to_all(normed, FRAME, split_axis=0, concat_axis=0, tiled=True)
    *blocks, spread = lax.optimization_barrier((*blocks, spread))
    gathered = assemble(place, blocks)
    spread = spread.reshape(frames, rows // frames, features)
    gathered_other = swap(gathered)
    attended = temporal_mine(place, spread, gathered)
    gathered_other, attended = lax.optimization_barrier((gathered_other, attended))
    updated = temporal_other(place, spread, gathered, gathered_other, attended)
    temporal_rows = lax.all_to_all(
        updated.reshape(rows, features), FRAME, split_axis=0, concat_axis=0, tiled=True
    )
    return (cross_rows[None], temporal_rows[None])


def solution(mesh):
    fine = Mesh(mesh.devices.reshape(2, 8, 4, 2, 2), ("xl", "z", "y", "xh", "c"))
    by_token = P(VIEW, FRAME + ("c",), None)
    placed = (by_token, P(), P(), P(VIEW, None), P(VIEW, None))
    return jax.shard_map(
        per_device,
        mesh=fine,
        in_specs=placed,
        out_specs=(by_token, by_token),
        check_vma=False,
    )
```

```python
import functools

import jax
import jax.numpy as jnp
from jax import lax
from jax.experimental import pallas as pl
from jax.experimental.pallas import tpu as pltpu
from jax.sharding import Mesh
from jax.sharding import PartitionSpec as P

HEADS = 16
HD = 64
PAIR = 2 * HD
QUAD = 4 * HD
LOG2E = 1.4426950408889634
CROSS_LIMIT = 24 * 1024 * 1024
UNROLL = 2
F32 = jnp.float32
BF16 = jnp.bfloat16


def dot(a, b):
    return jnp.dot(a, b, preferred_element_type=F32)


def layer_norm(rows):
    centred = rows - jnp.mean(rows, axis=-1, keepdims=True)
    variance = jnp.mean(centred * centred, axis=-1, keepdims=True)
    return (centred * lax.rsqrt(variance + 1e-06)).astype(BF16)


def lanes_of(width, index, rows=1):
    lane = lax.broadcasted_iota(jnp.int32, (rows, width), 1)
    return jnp.where(lane // HD == index, 1.0, 0.0).astype(BF16)


def project_blocks(x_refs, w_refs, norm_s, q_ref, kt_s, v_s):
    pairs, _, keys = kt_s.shape
    start = 0
    for x_ref in x_refs:
        norm_s[start : start + x_ref.shape[0], :] = layer_norm(x_ref[...].astype(F32))
        start += x_ref.shape[0]

    def project(which, quad):
        return dot(norm_s[...], w_refs[which][:, quad * QUAD : (quad + 1) * QUAD])

    for quad in range(pairs // 2):
        if q_ref is not None:
            made = (project(2, quad) * (HD**-0.5 * LOG2E)).astype(BF16)
            for part in range(2):
                q_ref[2 * quad + part] = made[:, part * PAIR : (part + 1) * PAIR]
        made = project(0, quad).astype(BF16)
        for part in range(2):
            kt_s[2 * quad + part] = made[:, part * PAIR : (part + 1) * PAIR].T
        made = project(1, quad).astype(BF16)
        for part in range(2):
            v_s[2 * quad + part, :, :PAIR] = made[:, part * PAIR : (part + 1) * PAIR]
            v_s[2 * quad + part, :, PAIR:] = jnp.ones((keys, PAIR), BF16)


def attend_pairs(q_ref, kt_s, v_s, state, outs, row_block, part=None):
    pairs, count = q_ref.shape[:2]
    begin, end = (0, count) if part is None else (part * count // 2, (part + 1) * count // 2)
    low = lax.broadcasted_iota(jnp.int32, (row_block, PAIR), 1) < HD

    def attend(pair, carry):
        transposed, values = kt_s[pair], v_s[pair]
        for start in range(begin, end, row_block):
            rows = slice(start, start + row_block)
            queries = q_ref[pair, rows, :]
            peaks, sums = [], []
            for head in range(2):
                scores = dot(queries * lanes_of(PAIR, head), transposed)
                peak = jnp.max(scores, axis=-1, keepdims=True)
                weights = jnp.exp2(scores - peak).astype(BF16)
                peaks.append(peak)
                sums.append(dot(weights, values))
            peak = jnp.where(low, peaks[0], peaks[1])
            result = jnp.where(low, sums[0][:, :PAIR], sums[1][:, :PAIR])
            total = jnp.where(low, sums[0][:, PAIR:], sums[1][:, PAIR:])
            if state is not None:
                o_in, m_in, l_in = state
                highest = jnp.maximum(peak, m_in[pair, rows, :])
                old, new = jnp.exp2(m_in[pair, rows, :] - highest), jnp.exp2(peak - highest)
                result = new * result + old * o_in[pair, rows, :]
                total = new * total + old * l_in[pair, rows, :]
                peak = highest
            if part is not None:
                offset = start - begin
                outs[0][pair, offset : offset + row_block, :] = (result / total).astype(BF16)
            else:
                for out, value in zip(outs, (result, peak, total)):
                    out[pair, rows, :] = value
        return carry

    lax.fori_loop(0, pairs, attend, 0, unroll=1 if state is None else UNROLL)


def project_kernel(x0_ref, x1_ref, wk_ref, wv_ref, wq_ref, q_ref, kt_ref, v_ref, norm_s):
    project_blocks((x0_ref, x1_ref), (wk_ref, wv_ref, wq_ref), norm_s, q_ref, kt_ref, v_ref)


def attend_kernel(row_block, q_ref, kt_ref, v_ref, *outs):
    attend_pairs(q_ref, kt_ref, v_ref, None, outs, row_block)


def project_more_kernel(blocks, *refs):
    x_refs, w_refs, (kt_ref, v_ref, norm_s) = refs[:blocks], refs[blocks:-3], refs[-3:]
    project_blocks(x_refs, w_refs, norm_s, None, kt_ref, v_ref)


def finish_kernel(row_block, part, q_ref, kt_ref, v_ref, o_ref, m_ref, l_ref, out_ref):
    attend_pairs(q_ref, kt_ref, v_ref, (o_ref, m_ref, l_ref), (out_ref,), row_block, part)


VMEM_SPEC = pl.BlockSpec(memory_space=pltpu.VMEM)
SMEM_SPEC = pl.BlockSpec(memory_space=pltpu.SMEM)


def local_kernel(kernel, name, operands, out_shape, scratch_shapes=(), scalars=0):
    return pl.pallas_call(
        kernel,
        in_specs=[SMEM_SPEC] * scalars + [VMEM_SPEC] * (len(operands) - scalars),
        out_specs=[VMEM_SPEC] * len(out_shape),
        scratch_shapes=list(scratch_shapes),
        out_shape=out_shape,
        compiler_params=pltpu.CompilerParams(vmem_limit_bytes=CROSS_LIMIT),
        cost_estimate=pl.CostEstimate(flops=10**6, bytes_accessed=10**5, transcendentals=0),
        name=name,
    )(*operands)


def cross_project(xs, weights):
    features, columns = weights[0].shape
    keys = sum(x.shape[0] for x in xs)
    pairs = columns // PAIR
    shapes = ((pairs, keys, PAIR), (pairs, PAIR, keys), (pairs, keys, 2 * PAIR))
    first = len(weights) == 3
    out_shape = [jax.ShapeDtypeStruct(shape, BF16) for shape in shapes[0 if first else 1 :]]
    scratch = [pltpu.VMEM((keys, features), BF16)]
    kernel = project_kernel if first else functools.partial(project_more_kernel, len(xs))
    name = "cross_project" if first else "cross_project_more"
    return local_kernel(kernel, name, (*xs, *weights), out_shape, scratch)


def cross_attend(queries, projected, state=None, part=None, row_block=384):
    pairs, count, width = queries.shape
    operands = (queries, *projected)
    if state is None:
        kept = [jax.ShapeDtypeStruct(queries.shape, F32)] * 3
        kernel = functools.partial(attend_kernel, row_block)
        return local_kernel(kernel, "cross_attend", operands, kept)
    out_shape = [jax.ShapeDtypeStruct((pairs, count // 2, width), BF16)]
    kernel = functools.partial(finish_kernel, row_block, part)
    return local_kernel(kernel, "cross_finish", (*operands, *state), out_shape)[0]


def cross_out_kernel(core_ref, mine_ref, other_ref, x_ref, w_ref, cross_ref, norm_ref):
    pairs = mine_ref.shape[0]
    half = pairs * PAIR
    made = None
    for ref, core in ((mine_ref, core_ref[0]), (other_ref, 1 - core_ref[0])):
        rows = jnp.concatenate([ref[pair] for pair in range(pairs)], axis=-1)
        part = dot(rows, w_ref[pl.ds(pl.multiple_of(core * half, half), half), :])
        made = part if made is None else made + part
    cross_ref[...] = made.astype(BF16)
    residual = x_ref[...].astype(F32) + cross_ref[...].astype(F32)
    norm_ref[...] = layer_norm(residual)


def cross_out(core, mine, other, tokens, w_cross_out):
    out_shape = [jax.ShapeDtypeStruct(tokens.shape, BF16)] * 2
    operands = (core, mine, other, tokens, w_cross_out)
    return local_kernel(cross_out_kernel, "cross_out", operands, out_shape, scalars=1)


GROUP = 16
BLOCKS = 16


def halves(ref, own_half):
    half = ref.shape[1] // 2
    return [
        ref[:, pl.ds(pl.multiple_of(which * half, half), half)]
        for which in (own_half, 1 - own_half)
    ]


def times(ref, w_ref, columns, own_half):
    block = w_ref.shape[0] // BLOCKS
    made = None
    for side, rows in enumerate(halves(ref, own_half)):
        starts = range(side * block, w_ref.shape[0], 2 * block)
        part = jnp.concatenate([w_ref[start : start + block, columns] for start in starts], axis=0)
        made = dot(rows, part) if made is None else made + dot(rows, part)
    return made


def grouped(shape):
    frames, positions, _ = shape
    for group in range(positions // GROUP):
        for frame in range(frames):
            start = (group * frames + frame) * GROUP
            yield slice(start, start + GROUP), frame, slice(group * GROUP, (group + 1) * GROUP)


def temporal_heads(x_ref, w_ref, own_half, x_s, store):
    frames, positions, features = x_ref.shape
    size = frames * GROUP
    half = features // 2
    heads = QUAD // HD
    for rows, frame, place in grouped(x_ref.shape):
        x_s[rows, :] = x_ref[frame, place, :]
    row = lax.broadcasted_iota(jnp.int32, (heads * size, size), 0)
    column = lax.broadcasted_iota(jnp.int32, (heads * size, size), 1)
    same = row % GROUP == column % GROUP
    head_of = lax.broadcasted_iota(jnp.int32, (size, QUAD), 1) // HD
    for quad in range(half // QUAD):

        def project(which):
            start = which * half + quad * QUAD
            return times(x_s, w_ref, slice(start, start + QUAD), own_half)

        queries = (project(0) * (HD**-0.5 * LOG2E)).astype(BF16)
        keys = project(1).astype(BF16)
        values = project(2).astype(BF16)
        for group in range(positions // GROUP):
            part = slice(group * size, (group + 1) * size)
            stacked = jnp.concatenate(
                [queries[part] * lanes_of(QUAD, head) for head in range(heads)], axis=0
            )
            scores = jnp.where(same, dot(stacked, keys[part].T), -jnp.inf)
            weights = jnp.exp2(scores - jnp.max(scores, axis=-1, keepdims=True))
            total = jnp.sum(weights, axis=-1, keepdims=True)
            result = dot(weights.astype(BF16), values[part]) / total
            attended = result[:size]
            for head in range(1, heads):
                attended = jnp.where(
                    head_of == head, result[head * size : (head + 1) * size], attended
                )
            store(part, quad * QUAD, attended.astype(BF16))


def temporal_attend_kernel(place_ref, x_ref, w_ref, att_ref, x_s):
    def store(rows, start, value):
        att_ref[rows, start : start + QUAD] = value

    temporal_heads(x_ref, w_ref, place_ref[1], x_s, store)


def temporal_out_kernel(place_ref, am_ref, ao_ref, wm_ref, wo_ref, out_ref, att_s):
    half = am_ref.shape[1]
    core, own_half = place_ref[0], place_ref[1]
    mine, other = pl.multiple_of(core * half, half), pl.multiple_of((1 - core) * half, half)
    att_s[:, pl.ds(mine, half)] = am_ref[...]
    att_s[:, pl.ds(other, half)] = ao_ref[...]
    for start, w_ref in ((mine, wm_ref), (other, wo_ref)):
        made = times(att_s, w_ref, slice(0, half), own_half).astype(BF16)
        for rows, frame, place in grouped(out_ref.shape):
            out_ref[frame, place, pl.ds(start, half)] = made[rows]


def assemble_kernel(place_ref, *refs):
    blocks, (qkv_ref, out_ref) = refs[:-2], refs[-2:]
    size = blocks[0].shape[0]
    count = out_ref.shape[0] // size
    cut = qkv_ref.shape[1]
    for ref, step in zip(blocks, (0, -1, 1, -2, 2, -3, 3, 4)):
        index = lax.rem(place_ref[2] + step + count, count)
        rows = pl.ds(pl.multiple_of(index * size, size), size)
        qkv_ref[rows, :] = ref[:, :cut]
        out_ref[rows, :] = ref[:, cut:]


def assemble(place, blocks):
    size, columns = blocks[0].shape
    rows, cut = 8 * size, columns // 4 * 3
    out_shape = [jax.ShapeDtypeStruct((rows, width), BF16) for width in (cut, columns - cut)]
    return local_kernel(assemble_kernel, "assemble", (place, *blocks), out_shape, (), 1)


def temporal_attend(place, rows, weights):
    frames, positions, features = rows.shape
    count = frames * positions
    out_shape = [jax.ShapeDtypeStruct((count, features // 2), BF16)]
    scratch = [pltpu.VMEM((count, features), BF16)]
    operands = (place, rows, weights)
    return local_kernel(
        temporal_attend_kernel, "temporal_attend", operands, out_shape, scratch, 1
    )[0]


def temporal_out(place, shape, mine, other, w_mine, w_other):
    out_shape = [jax.ShapeDtypeStruct(shape, BF16)]
    scratch = [pltpu.VMEM((mine.shape[0], shape[2]), BF16)]
    operands = (place, mine, other, w_mine, w_other)
    return local_kernel(temporal_out_kernel, "temporal_out", operands, out_shape, scratch, 1)[0]


VIEW = ("xl", "z")
FRAME = ("y", "xh")
SWAP = [(0, 1), (1, 0)]


def across(value):
    pairs = []
    for xl in range(2):
        for xh in range(2):
            for core in range(2):
                target = (1 - xl) * 4 + (xh ^ core) * 2 + core
                pairs.append((xl * 4 + xh * 2 + core, target))
    return lax.ppermute(value, ("xl", "xh", "c"), pairs)


def along(value, steps):
    return lax.ppermute(value, "z", [(i, (i + steps) % 8) for i in range(8)])


def opposite(ahead, behind):
    value = jnp.where(lax.axis_index("c") == 0, ahead, behind)
    pairs = []
    for z in range(8):
        pairs += [(2 * z, (z + 1) % 8 * 2), (2 * z + 1, (z - 1) % 8 * 2 + 1)]
    return lax.ppermute(value, ("z", "c"), pairs)


def per_device(tokens, w_cross_qkv, w_cross_out, w_temporal_qkv, w_temporal_out):
    own = tokens[0]
    rows, features = own.shape
    half = features // 2
    core_index = lax.axis_index("c")
    core = core_index.astype(jnp.int32).reshape(1)
    place = jnp.stack([core_index, lax.axis_index("xl"), lax.axis_index("z")]).astype(jnp.int32)
    views = lax.axis_size(VIEW)
    forward = [(i, (i + 1) % views) for i in range(views)]
    backward = [(i, (i - 1) % views) for i in range(views)]

    swap = lambda value: lax.ppermute(value, "c", SWAP)
    partner = swap(own)
    before, after = (lax.ppermute(own, VIEW, pairs) for pairs in (forward, backward))

    sides = [
        jnp.concatenate(
            [
                w[:, start + side * half : start + (side + 1) * half]
                for w, start in (
                    (w_temporal_qkv, 0),
                    (w_temporal_qkv, features),
                    (w_temporal_qkv, 2 * features),
                    (w_temporal_out, 0),
                )
            ],
            axis=1,
        )
        for side in range(2)
    ]
    shard = jnp.where(core_index == 0, sides[0], sides[1])
    w_query, w_key, w_value = (
        lax.dynamic_slice_in_dim(w_cross_qkv, which * features + core_index * half, half, 1)
        for which in range(3)
    )
    weights = (w_key, w_value)
    queries, *projected = cross_project((own, partner), (*weights, w_query))
    shard, queries = lax.optimization_barrier((shard, queries))
    blocks = [jnp.concatenate([shard, across(shard)], axis=0)]
    blocks += [along(blocks[0], 1), along(blocks[0], -1)]
    state = list(cross_attend(queries, projected))
    before, after, state[0] = lax.optimization_barrier((before, after, state[0]))
    arrived = (before, after, swap(before), swap(after))
    projected = cross_project(arrived, weights)
    theirs = cross_attend(queries, projected, state, part=1)
    blocks[1], blocks[2], theirs = lax.optimization_barrier((blocks[1], blocks[2], theirs))
    blocks += [along(blocks[1], 1), along(blocks[2], -1)]
    other = swap(theirs)
    mine = cross_attend(queries, projected, state, part=0)
    *blocks, other, mine = lax.optimization_barrier((*blocks, other, mine))
    cross_rows, normed = cross_out(core, mine, other, own, w_cross_out)

    blocks += [along(blocks[3], 1), along(blocks[4], -1)]
    blocks += [opposite(blocks[5], blocks[6])]
    frames = lax.axis_size(FRAME)
    spread = lax.all_to_all(normed, FRAME, split_axis=0, concat_axis=0, tiled=True)
    *blocks, spread = lax.optimization_barrier((*blocks, spread))
    gathered, out_gathered = assemble(place, blocks)
    spread = spread.reshape(frames, rows // frames, features)
    gathered_other, out_other = swap(gathered), swap(out_gathered)
    attended = temporal_attend(place, spread, gathered)
    gathered_other, attended = lax.optimization_barrier((gathered_other, attended))
    attended_other = temporal_attend(place, spread, gathered_other)
    out_other, attended_other = lax.optimization_barrier((out_other, attended_other))
    updated = temporal_out(
        place, spread.shape, attended, attended_other, out_gathered, out_other
    )
    temporal_rows = lax.all_to_all(
        updated.reshape(rows, features), FRAME, split_axis=0, concat_axis=0, tiled=True
    )
    return (cross_rows[None], temporal_rows[None])


def solution(mesh):
    fine = Mesh(mesh.devices.reshape(2, 8, 4, 2, 2), ("xl", "z", "y", "xh", "c"))
    by_token = P(VIEW, FRAME + ("c",), None)
    placed = (by_token, P(), P(), P(VIEW, None), P(VIEW, None))
    return jax.shard_map(
        per_device,
        mesh=fine,
        in_specs=placed,
        out_specs=(by_token, by_token),
        check_vma=False,
    )
```

```python
import functools

import jax
import jax.numpy as jnp
from jax import lax
from jax.experimental import pallas as pl
from jax.experimental.pallas import tpu as pltpu
from jax.sharding import Mesh
from jax.sharding import PartitionSpec as P

HEADS = 16
HD = 64
PAIR = 2 * HD
QUAD = 4 * HD
LOG2E = 1.4426950408889634
CROSS_LIMIT = 24 * 1024 * 1024
UNROLL = 2
F32 = jnp.float32
BF16 = jnp.bfloat16


def dot(a, b):
    return jnp.dot(a, b, preferred_element_type=F32)


def layer_norm(rows):
    centred = rows - jnp.mean(rows, axis=-1, keepdims=True)
    variance = jnp.mean(centred * centred, axis=-1, keepdims=True)
    return (centred * lax.rsqrt(variance + 1e-06)).astype(BF16)


def lanes_of(width, index, rows=1):
    lane = lax.broadcasted_iota(jnp.int32, (rows, width), 1)
    return jnp.where(lane // HD == index, 1.0, 0.0).astype(BF16)


def project_blocks(x_refs, w_refs, norm_s, q_ref, kt_s, v_s):
    pairs, _, keys = kt_s.shape
    start = 0
    for x_ref in x_refs:
        norm_s[start : start + x_ref.shape[0], :] = layer_norm(x_ref[...].astype(F32))
        start += x_ref.shape[0]

    def project(which, quad):
        return dot(norm_s[...], w_refs[which][:, quad * QUAD : (quad + 1) * QUAD])

    for quad in range(pairs // 2):
        if q_ref is not None:
            made = (project(2, quad) * (HD**-0.5 * LOG2E)).astype(BF16)
            for part in range(2):
                q_ref[2 * quad + part] = made[:, part * PAIR : (part + 1) * PAIR]
        made = project(0, quad).astype(BF16)
        for part in range(2):
            kt_s[2 * quad + part] = made[:, part * PAIR : (part + 1) * PAIR].T
        made = project(1, quad).astype(BF16)
        for part in range(2):
            v_s[2 * quad + part, :, :PAIR] = made[:, part * PAIR : (part + 1) * PAIR]
            v_s[2 * quad + part, :, PAIR:] = jnp.ones((keys, PAIR), BF16)


def attend_pairs(q_ref, kt_s, v_s, state, outs, row_block, part=None):
    pairs, count = q_ref.shape[:2]
    begin, end = (0, count) if part is None else (part * count // 2, (part + 1) * count // 2)
    low = lax.broadcasted_iota(jnp.int32, (row_block, PAIR), 1) < HD

    def attend(pair, carry):
        transposed, values = kt_s[pair], v_s[pair]
        for start in range(begin, end, row_block):
            rows = slice(start, start + row_block)
            queries = q_ref[pair, rows, :]
            peaks, sums = [], []
            for head in range(2):
                scores = dot(queries * lanes_of(PAIR, head), transposed)
                peak = jnp.max(scores, axis=-1, keepdims=True)
                weights = jnp.exp2(scores - peak).astype(BF16)
                peaks.append(peak)
                sums.append(dot(weights, values))
            peak = jnp.where(low, peaks[0], peaks[1])
            result = jnp.where(low, sums[0][:, :PAIR], sums[1][:, :PAIR])
            total = jnp.where(low, sums[0][:, PAIR:], sums[1][:, PAIR:])
            if state is not None:
                o_in, m_in, l_in = state
                highest = jnp.maximum(peak, m_in[pair, rows, :])
                old, new = jnp.exp2(m_in[pair, rows, :] - highest), jnp.exp2(peak - highest)
                result = new * result + old * o_in[pair, rows, :]
                total = new * total + old * l_in[pair, rows, :]
                peak = highest
            if part is not None:
                offset = start - begin
                outs[0][pair, offset : offset + row_block, :] = (result / total).astype(BF16)
            else:
                for out, value in zip(outs, (result, peak, total)):
                    out[pair, rows, :] = value
        return carry

    lax.fori_loop(0, pairs, attend, 0, unroll=1 if state is None else pairs if part == 0 else UNROLL)


def project_kernel(x0_ref, x1_ref, wk_ref, wv_ref, wq_ref, q_ref, kt_ref, v_ref, norm_s):
    project_blocks((x0_ref, x1_ref), (wk_ref, wv_ref, wq_ref), norm_s, q_ref, kt_ref, v_ref)


def attend_kernel(row_block, q_ref, kt_ref, v_ref, *outs):
    attend_pairs(q_ref, kt_ref, v_ref, None, outs, row_block)


def project_more_kernel(blocks, *refs):
    x_refs, w_refs, (kt_ref, v_ref, norm_s) = refs[:blocks], refs[blocks:-3], refs[-3:]
    project_blocks(x_refs, w_refs, norm_s, None, kt_ref, v_ref)


def finish_kernel(row_block, part, q_ref, kt_ref, v_ref, o_ref, m_ref, l_ref, out_ref):
    attend_pairs(q_ref, kt_ref, v_ref, (o_ref, m_ref, l_ref), (out_ref,), row_block, part)


VMEM_SPEC = pl.BlockSpec(memory_space=pltpu.VMEM)
SMEM_SPEC = pl.BlockSpec(memory_space=pltpu.SMEM)


def local_kernel(kernel, name, operands, out_shape, scratch_shapes=(), scalars=0):
    return pl.pallas_call(
        kernel,
        in_specs=[SMEM_SPEC] * scalars + [VMEM_SPEC] * (len(operands) - scalars),
        out_specs=[VMEM_SPEC] * len(out_shape),
        scratch_shapes=list(scratch_shapes),
        out_shape=out_shape,
        compiler_params=pltpu.CompilerParams(vmem_limit_bytes=CROSS_LIMIT),
        cost_estimate=pl.CostEstimate(flops=10**6, bytes_accessed=10**5, transcendentals=0),
        name=name,
    )(*operands)


def cross_project(xs, weights):
    features, columns = weights[0].shape
    keys = sum(x.shape[0] for x in xs)
    pairs = columns // PAIR
    shapes = ((pairs, keys, PAIR), (pairs, PAIR, keys), (pairs, keys, 2 * PAIR))
    first = len(weights) == 3
    out_shape = [jax.ShapeDtypeStruct(shape, BF16) for shape in shapes[0 if first else 1 :]]
    scratch = [pltpu.VMEM((keys, features), BF16)]
    kernel = project_kernel if first else functools.partial(project_more_kernel, len(xs))
    name = "cross_project" if first else "cross_project_more"
    return local_kernel(kernel, name, (*xs, *weights), out_shape, scratch)


def cross_attend(queries, projected, state=None, part=None, row_block=384):
    pairs, count, width = queries.shape
    operands = (queries, *projected)
    if state is None:
        kept = [jax.ShapeDtypeStruct(queries.shape, F32)] * 3
        kernel = functools.partial(attend_kernel, row_block)
        return local_kernel(kernel, "cross_attend", operands, kept)
    out_shape = [jax.ShapeDtypeStruct((pairs, count // 2, width), BF16)]
    kernel = functools.partial(finish_kernel, row_block, part)
    return local_kernel(kernel, "cross_finish", (*operands, *state), out_shape)[0]


def cross_out_kernel(core_ref, mine_ref, other_ref, x_ref, w_ref, cross_ref, norm_ref):
    pairs = mine_ref.shape[0]
    half = pairs * PAIR
    made = None
    for ref, core in ((mine_ref, core_ref[0]), (other_ref, 1 - core_ref[0])):
        rows = jnp.concatenate([ref[pair] for pair in range(pairs)], axis=-1)
        part = dot(rows, w_ref[pl.ds(pl.multiple_of(core * half, half), half), :])
        made = part if made is None else made + part
    cross_ref[...] = made.astype(BF16)
    residual = x_ref[...].astype(F32) + cross_ref[...].astype(F32)
    norm_ref[...] = layer_norm(residual)


def cross_out(core, mine, other, tokens, w_cross_out):
    out_shape = [jax.ShapeDtypeStruct(tokens.shape, BF16)] * 2
    operands = (core, mine, other, tokens, w_cross_out)
    return local_kernel(cross_out_kernel, "cross_out", operands, out_shape, scalars=1)


GROUP = 16
BLOCKS = 16


def halves(ref, own_half):
    half = ref.shape[1] // 2
    return [
        ref[:, pl.ds(pl.multiple_of(which * half, half), half)]
        for which in (own_half, 1 - own_half)
    ]


def times(ref, w_ref, columns, own_half):
    block = w_ref.shape[0] // BLOCKS
    made = None
    for side, rows in enumerate(halves(ref, own_half)):
        starts = range(side * block, w_ref.shape[0], 2 * block)
        part = jnp.concatenate([w_ref[start : start + block, columns] for start in starts], axis=0)
        made = dot(rows, part) if made is None else made + dot(rows, part)
    return made


def grouped(shape):
    frames, positions, _ = shape
    for group in range(positions // GROUP):
        for frame in range(frames):
            start = (group * frames + frame) * GROUP
            yield slice(start, start + GROUP), frame, slice(group * GROUP, (group + 1) * GROUP)


def temporal_heads(x_ref, w_ref, own_half, x_s, store):
    frames, positions, features = x_ref.shape
    size = frames * GROUP
    half = features // 2
    heads = QUAD // HD
    for rows, frame, place in grouped(x_ref.shape):
        x_s[rows, :] = x_ref[frame, place, :]
    row = lax.broadcasted_iota(jnp.int32, (heads * size, size), 0)
    column = lax.broadcasted_iota(jnp.int32, (heads * size, size), 1)
    same = row % GROUP == column % GROUP
    head_of = lax.broadcasted_iota(jnp.int32, (size, QUAD), 1) // HD
    for quad in range(half // QUAD):

        def project(which):
            start = which * half + quad * QUAD
            return times(x_s, w_ref, slice(start, start + QUAD), own_half)

        queries = (project(0) * (HD**-0.5 * LOG2E)).astype(BF16)
        keys = project(1).astype(BF16)
        values = project(2).astype(BF16)
        for group in range(positions // GROUP):
            part = slice(group * size, (group + 1) * size)
            stacked = jnp.concatenate(
                [queries[part] * lanes_of(QUAD, head) for head in range(heads)], axis=0
            )
            scores = jnp.where(same, dot(stacked, keys[part].T), -jnp.inf)
            weights = jnp.exp2(scores - jnp.max(scores, axis=-1, keepdims=True))
            total = jnp.sum(weights, axis=-1, keepdims=True)
            result = dot(weights.astype(BF16), values[part]) / total
            attended = result[:size]
            for head in range(1, heads):
                attended = jnp.where(
                    head_of == head, result[head * size : (head + 1) * size], attended
                )
            store(part, quad * QUAD, attended.astype(BF16))


def temporal_attend_kernel(place_ref, x_ref, w_ref, att_ref, x_s):
    def store(rows, start, value):
        att_ref[rows, start : start + QUAD] = value

    temporal_heads(x_ref, w_ref, place_ref[1], x_s, store)


def temporal_out_kernel(place_ref, am_ref, ao_ref, wm_ref, wo_ref, out_ref, att_s):
    half = am_ref.shape[1]
    core, own_half = place_ref[0], place_ref[1]
    mine, other = pl.multiple_of(core * half, half), pl.multiple_of((1 - core) * half, half)
    att_s[:, pl.ds(mine, half)] = am_ref[...]
    att_s[:, pl.ds(other, half)] = ao_ref[...]
    for start, w_ref in ((mine, wm_ref), (other, wo_ref)):
        made = times(att_s, w_ref, slice(0, half), own_half).astype(BF16)
        for rows, frame, place in grouped(out_ref.shape):
            out_ref[frame, place, pl.ds(start, half)] = made[rows]


def assemble_kernel(place_ref, *refs):
    blocks, (qkv_ref, out_ref) = refs[:-2], refs[-2:]
    size = blocks[0].shape[0]
    count = out_ref.shape[0] // size
    cut = qkv_ref.shape[1]
    for ref, step in zip(blocks, (0, -1, 1, -2, 2, -3, 3, 4)):
        index = lax.rem(place_ref[2] + step + count, count)
        rows = pl.ds(pl.multiple_of(index * size, size), size)
        qkv_ref[rows, :] = ref[:, :cut]
        out_ref[rows, :] = ref[:, cut:]


def assemble(place, blocks):
    size, columns = blocks[0].shape
    rows, cut = 8 * size, columns // 4 * 3
    out_shape = [jax.ShapeDtypeStruct((rows, width), BF16) for width in (cut, columns - cut)]
    return local_kernel(assemble_kernel, "assemble", (place, *blocks), out_shape, (), 1)


def temporal_attend(place, rows, weights):
    frames, positions, features = rows.shape
    count = frames * positions
    out_shape = [jax.ShapeDtypeStruct((count, features // 2), BF16)]
    scratch = [pltpu.VMEM((count, features), BF16)]
    operands = (place, rows, weights)
    return local_kernel(
        temporal_attend_kernel, "temporal_attend", operands, out_shape, scratch, 1
    )[0]


def temporal_out(place, shape, mine, other, w_mine, w_other):
    out_shape = [jax.ShapeDtypeStruct(shape, BF16)]
    scratch = [pltpu.VMEM((mine.shape[0], shape[2]), BF16)]
    operands = (place, mine, other, w_mine, w_other)
    return local_kernel(temporal_out_kernel, "temporal_out", operands, out_shape, scratch, 1)[0]


VIEW = ("xl", "z")
FRAME = ("y", "xh")
SWAP = [(0, 1), (1, 0)]


def across(value):
    pairs = []
    for xl in range(2):
        for xh in range(2):
            for core in range(2):
                target = (1 - xl) * 4 + (xh ^ core) * 2 + core
                pairs.append((xl * 4 + xh * 2 + core, target))
    return lax.ppermute(value, ("xl", "xh", "c"), pairs)


def along(value, steps):
    return lax.ppermute(value, "z", [(i, (i + steps) % 8) for i in range(8)])


def opposite(ahead, behind):
    value = jnp.where(lax.axis_index("c") == 0, ahead, behind)
    pairs = []
    for z in range(8):
        pairs += [(2 * z, (z + 1) % 8 * 2), (2 * z + 1, (z - 1) % 8 * 2 + 1)]
    return lax.ppermute(value, ("z", "c"), pairs)


def per_device(tokens, w_cross_qkv, w_cross_out, w_temporal_qkv, w_temporal_out):
    own = tokens[0]
    rows, features = own.shape
    half = features // 2
    core_index = lax.axis_index("c")
    core = core_index.astype(jnp.int32).reshape(1)
    place = jnp.stack([core_index, lax.axis_index("xl"), lax.axis_index("z")]).astype(jnp.int32)
    views = lax.axis_size(VIEW)
    forward = [(i, (i + 1) % views) for i in range(views)]
    backward = [(i, (i - 1) % views) for i in range(views)]

    swap = lambda value: lax.ppermute(value, "c", SWAP)
    partner = swap(own)
    before, after = (lax.ppermute(own, VIEW, pairs) for pairs in (forward, backward))

    sides = [
        jnp.concatenate(
            [
                w[:, start + side * half : start + (side + 1) * half]
                for w, start in (
                    (w_temporal_qkv, 0),
                    (w_temporal_qkv, features),
                    (w_temporal_qkv, 2 * features),
                    (w_temporal_out, 0),
                )
            ],
            axis=1,
        )
        for side in range(2)
    ]
    shard = jnp.where(core_index == 0, sides[0], sides[1])
    w_query, w_key, w_value = (
        lax.dynamic_slice_in_dim(w_cross_qkv, which * features + core_index * half, half, 1)
        for which in range(3)
    )
    weights = (w_key, w_value)
    queries, *projected = cross_project((own, partner), (*weights, w_query))
    shard, queries = lax.optimization_barrier((shard, queries))
    blocks = [jnp.concatenate([shard, across(shard)], axis=0)]
    blocks += [along(blocks[0], 1), along(blocks[0], -1)]
    state = list(cross_attend(queries, projected))
    before, after, state[0] = lax.optimization_barrier((before, after, state[0]))
    arrived = (before, after, swap(before), swap(after))
    projected = cross_project(arrived, weights)
    theirs = cross_attend(queries, projected, state, part=1)
    blocks[1], blocks[2], theirs = lax.optimization_barrier((blocks[1], blocks[2], theirs))
    blocks += [along(blocks[1], 1), along(blocks[2], -1)]
    other = swap(theirs)
    mine = cross_attend(queries, projected, state, part=0)
    *blocks, other, mine = lax.optimization_barrier((*blocks, other, mine))
    cross_rows, normed = cross_out(core, mine, other, own, w_cross_out)

    blocks += [along(blocks[3], 1), along(blocks[4], -1)]
    blocks += [opposite(blocks[5], blocks[6])]
    frames = lax.axis_size(FRAME)
    spread = lax.all_to_all(normed, FRAME, split_axis=0, concat_axis=0, tiled=True)
    *blocks, spread = lax.optimization_barrier((*blocks, spread))
    gathered, out_gathered = assemble(place, blocks)
    spread = spread.reshape(frames, rows // frames, features)
    gathered_other, out_other = swap(gathered), swap(out_gathered)
    attended = temporal_attend(place, spread, gathered)
    gathered_other, attended = lax.optimization_barrier((gathered_other, attended))
    attended_other = temporal_attend(place, spread, gathered_other)
    out_other, attended_other = lax.optimization_barrier((out_other, attended_other))
    updated = temporal_out(
        place, spread.shape, attended, attended_other, out_gathered, out_other
    )
    temporal_rows = lax.all_to_all(
        updated.reshape(rows, features), FRAME, split_axis=0, concat_axis=0, tiled=True
    )
    return (cross_rows[None], temporal_rows[None])


def solution(mesh):
    fine = Mesh(mesh.devices.reshape(2, 8, 4, 2, 2), ("xl", "z", "y", "xh", "c"))
    by_token = P(VIEW, FRAME + ("c",), None)
    placed = (by_token, P(), P(), P(VIEW, None), P(VIEW, None))
    return jax.shard_map(
        per_device,
        mesh=fine,
        in_specs=placed,
        out_specs=(by_token, by_token),
        check_vma=False,
    )
```
